512 devices in a mesh: dp: 8 (over y, core), fsdp: 16 (over z), tensor: 4 (over x).
Axes of the slice: x: 4, y: 4, z: 16, core: 2. Of those that a mesh axis runs over, the one named last changes fastest.
Arguments:
- weight: float32 [4096, 4096], P('fsdp', 'tensor'), may hold values from -0.000234375 to 0.000234375
- momentum: bfloat16 [8, 4096, 4096], P('dp', 'fsdp', 'tensor'), may hold values from -8 to 8
- grads: bfloat16 [8, 2, 4096, 4096], P('dp', None, 'fsdp', 'tensor'), may hold values from -8 to 8
- right_factor: float32 [64, 4096], P(None, 'tensor'), may hold values from -1 to 1
Outputs:
- new_weight: float32 [4096, 4096], P('fsdp', 'tensor')
- new_momentum: bfloat16 [8, 4096, 4096], P('dp', 'fsdp', 'tensor')
- new_right: float32 [64, 4096], P(None, 'tensor')
The draws below stay inside these ranges and needn't reach their ends.
All inputs are finite; a program needn't handle non-finite values.
Results may differ from the reference program's by a relative error of at most 0.001.
Values sent between devices are 32-bit elements; how exact they have to be, the bound alone decides.
A program may use at most 64 MiB of HBM per device.

```python
import math
import jax
import jax.numpy as jnp
from jax import lax

ROWS = 4096
COLS = 4096
RANK = 64
LOOPS = 2
REPLICAS = 8


noise_level = 0.35


def shared_basis(key):
    base = jax.random.fold_in(key, 101)
    subkeys = jax.random.split(base, 3)
    columns = jax.random.normal(subkeys[0], (ROWS, RANK), jnp.float32)
    basis_rows = jax.random.normal(subkeys[1], (RANK, COLS), jnp.float32)
    mixing = jax.random.normal(subkeys[2], (RANK, RANK), jnp.float32) * (0.25 / math.sqrt(RANK))
    return (columns, basis_rows, mixing)


def structured(key, marker, number):
    columns, basis_rows, mixing = shared_basis(key)
    subkeys = jax.random.split(jax.random.fold_in(key, marker), 3)
    scales = jnp.exp(jax.random.uniform(subkeys[0], (number, RANK), jnp.float32, -1.0, 1.0))
    own_part = jax.random.normal(subkeys[1], (number, RANK, RANK), jnp.float32) * (0.2 / math.sqrt(RANK))
    cores = own_part + mixing[None] + scales[:, :, None] * jnp.eye(RANK, dtype=jnp.float32)[None]
    noise_keys = jax.random.split(subkeys[2], number)

    def single(entry):
        core, noise_key = entry
        lowrank = jnp.dot(jnp.dot(columns, core), basis_rows) / math.sqrt(2 * RANK)
        noise = jax.random.normal(noise_key, (ROWS, COLS), jnp.float32) * noise_level
        return jnp.clip(lowrank + noise, -8.0, 8.0)
    return lax.map(single, (cores, noise_keys))


def draw_momentum(key, part):
    return structured(key, 1, REPLICAS).astype(jnp.bfloat16)


def draw_grads(key, part):
    values = structured(key, 2, REPLICAS * LOOPS)
    return values.reshape(REPLICAS, LOOPS, ROWS, COLS).astype(jnp.bfloat16)


def draw_right_factor(key, part):
    columns, basis_rows, mixing = shared_basis(key)
    subkeys = jax.random.split(jax.random.fold_in(key, 3), 3)
    jitter = jax.random.normal(subkeys[0], (RANK, COLS), jnp.float32)
    weights_common = jax.random.normal(subkeys[1], (RANK,), jnp.float32)
    common = jnp.dot(weights_common, basis_rows) / math.sqrt(RANK)
    lowest = -4.2
    spread = jnp.exp(jax.random.uniform(subkeys[2], (RANK, 1), jnp.float32, lowest, 0.0))
    blended_rows = common[None, :] + spread * (basis_rows + 0.5 * jitter)
    return blended_rows / jnp.sqrt(jnp.sum(blended_rows * blended_rows, axis=1, keepdims=True))


def steps_of(key, shape, cuts, smallest, largest):
    loudness = 1.0
    for dim, blocks in cuts:
        steps = jax.random.uniform(jax.random.fold_in(jax.random.fold_in(key, 6), dim), (blocks,), jnp.float32, smallest / len(cuts), largest / len(cuts))
        loudness = loudness * jnp.repeat(jnp.exp(steps), shape[dim] // blocks).reshape((-1,) + (1,) * (len(shape) - 1 - dim))
    return loudness


def centred(rng, extent, scale, bound, cuts=(), held_as=jnp.bfloat16):
    drawn = jax.random.normal(rng, extent, jnp.float32) * scale
    if len(cuts) > 0:
        drawn = steps_of(rng, extent, cuts, -0.22, 0.18) * drawn
    return jnp.clip(drawn, min=-bound, max=bound).astype(held_as)


def setup_inputs(seed: int = 0) -> dict:
    keys = jax.random.split(jax.random.key(seed), 5)
    weight = centred(keys[0], (ROWS, COLS), (0.02 * RANK ** 0.5 * COLS ** -1), 0.000234375, ((0, 16), (1, 4)), jnp.float32)
    momentum = draw_momentum(jax.random.fold_in(keys[4], 71), 0)
    grads = draw_grads(jax.random.fold_in(keys[4], 71), 0)
    right_factor = draw_right_factor(jax.random.fold_in(keys[4], 71), 0)
    return dict(weight=weight, momentum=momentum, grads=grads, right_factor=right_factor)


decay_part = 0.05
learn_rate = 0.02
epsilon = 1e-06

def orthonormal(factor):
    for sweep in range(2):
        gram = jnp.dot(factor.T.astype(jnp.float32), factor.astype(jnp.float32), precision=lax.Precision.HIGHEST, preferred_element_type=jnp.float32)
        lower = jnp.linalg.cholesky(gram)
        factor = jax.scipy.linalg.solve_triangular(lower, factor.T, lower=True).T
    return factor

def reference(weight, momentum, grads, right_factor):
    replicas = momentum.shape[0]
    blended = momentum.astype(jnp.float32) + lax.optimization_barrier(jnp.sum(grads.astype(jnp.float32), axis=1))
    left_raw = jnp.einsum('irc,kc->rk', blended, right_factor, precision=lax.Precision.HIGHEST) / replicas
    left = orthonormal(left_raw)
    right = jnp.einsum('irc,rk->ikc', blended, left, precision=lax.Precision.HIGHEST)
    new_momentum = (blended - decay_part * jnp.einsum('rk,ikc->irc', left, right, precision=lax.Precision.HIGHEST)).astype(jnp.bfloat16)
    shared = lax.optimization_barrier(jnp.sum(right, axis=0)) / replicas
    norms = jnp.sqrt(lax.optimization_barrier(jnp.sum(shared * shared, axis=1, keepdims=True)) + epsilon)
    new_right = shared / norms
    scale = learn_rate * math.sqrt(ROWS / COLS)
    new_weight = weight - scale * jnp.dot(left.astype(jnp.float32), new_right.astype(jnp.float32), precision=lax.Precision.HIGHEST, preferred_element_type=jnp.float32)
    return (new_weight, new_momentum, new_right)
```

```python
import functools
import math

import jax
import jax.numpy as jnp
from jax import lax
from jax.experimental import pallas as pl
from jax.experimental.pallas import tpu as pltpu
from jax.sharding import PartitionSpec as P

ROWS = 4096
COLS = 4096

decay_part = 0.05
learn_rate = 0.02
epsilon = 1e-06

MESH = pl.DeviceIdType.MESH
f32 = jnp.float32
bf16 = jnp.bfloat16
NN = (((1,), (0,)), ((), ()))
NT = (((1,), (1,)), ((), ()))


def split(x, n):
    parts = []
    for k in range(n):
        part = x.astype(bf16)
        parts.append(part)
        if k < n - 1:
            x = x - part.astype(f32)
    return parts


def dots(a, b, dims, order):
    total = None
    pairs = [(i, j) for i in range(len(a)) for j in range(len(b)) if i + j < order]
    for i, j in sorted(pairs, key=lambda t: -(t[0] + t[1])):
        term = lax.dot_general(a[i], b[j], dims, preferred_element_type=f32)
        total = term if total is None else total + term
    return total


def row_of(v, j):
    return jnp.broadcast_to(v[j : j + 1, :], (8, 128))


def lane_of(v, j):
    return jnp.broadcast_to(v[:, j : j + 1], (8, 128))


def eliminate(ref):
    sub = lax.broadcasted_iota(jnp.int32, (8, 128), 0)

    def body(kb, _):
        o = pl.multiple_of(kb * 8, 8)
        shift = lax.rem(128 - 8 * kb, 128)
        R = ref[pl.ds(o, 8), :]
        W = [R] + [ref[8 * i : 8 * i + 8, :] for i in range(1, 8)]
        D = [pltpu.roll(w, shift, 1) for w in W]
        C = [[lane_of(d, j) for j in range(8)] for d in D]
        Ls = [[None] * 8 for _ in range(8)]
        us = []
        for j in range(8):
            r = lax.rsqrt(row_of(C[0][j], j))
            for i in range(8):
                Ls[i][j] = C[i][j] * r
            u = row_of(R, j) * r
            us.append(u)
            R = R - Ls[0][j] * u
            for k in range(j + 1, 8):
                s = row_of(Ls[0][j], k)
                for i in range(8):
                    C[i][k] = C[i][k] - Ls[i][j] * s
        U = us[0]
        for j in range(1, 8):
            U = jnp.where(sub == j, us[j], U)
        for i in range(1, 8):
            w = W[i]
            for j in range(8):
                w = w - Ls[i][j] * us[j]
            ref[8 * i : 8 * i + 8, :] = jnp.where(i > kb, w, W[i])
        ref[pl.ds(o, 8), :] = U
        return 0

    lax.fori_loop(0, 8, body, 0)


def kernel(
    w_hbm, m_hbm, g_hbm, r_hbm, nw_hbm, nm_hbm, nr_hbm,
    w_v, m_v, g_v, r_v, bhi, blo,
    pc_send, pc_recv, p_send, p_recv, pk, qk,
    rr, rr_recv, rr_all, d_recv, sd, sd_recv, s_sub, s_all,
    gy, gx, hy, hx, aug, sq,
    nw_v, nm_v, nr_v,
    in_sem, out_sem, ssem, rsem,
):
    dp = lax.axis_index("dp")
    z = lax.axis_index("fsdp")
    x = lax.axis_index("tensor")
    y = dp // 2
    core = lax.rem(dp, 2)
    q = y * 4 + x

    loads = [
        pltpu.make_async_copy(m_hbm.at[0], m_v, in_sem.at[0]),
        pltpu.make_async_copy(g_hbm.at[0], g_v, in_sem.at[1]),
        pltpu.make_async_copy(r_hbm, r_v, in_sem.at[2]),
        pltpu.make_async_copy(w_hbm, w_v, in_sem.at[3]),
    ]
    for load in loads:
        load.start()

    mate = {"dp": y * 2 + 1 - core}
    plane = []
    for d in range(1, 16):
        o = lax.rem(q + d, 16)
        plane.append((o, {"dp": (o // 4) * 2 + core, "tensor": lax.rem(o, 4)}))
    column = []
    for d in range(1, 16):
        o = lax.rem(z + d, 16)
        column.append((o, {"fsdp": o}))
    replicas = []
    for d in range(1, 8):
        o = lax.rem(dp + d, 8)
        replicas.append((o, {"dp": o}))
    ys, xs = [], []
    for d in range(1, 4):
        o = lax.rem(y + d, 4)
        ys.append((o, {"dp": o * 2 + core}))
        o = lax.rem(x + d, 4)
        xs.append((o, {"tensor": o}))

    barrier = pltpu.get_barrier_semaphore()
    greeted = [mate] + [p for _, p in plane] + [p for _, p in column]
    for d in range(1, 4):
        greeted.append({"dp": lax.rem(y + d, 4) * 2 + 1 - core})
    for p in greeted:
        pl.semaphore_signal(barrier, inc=1, device_id=p, device_id_type=MESH)

    def send(phase, src, dst, peer):
        pltpu.make_async_remote_copy(
            src_ref=src, dst_ref=dst, send_sem=ssem.at[phase], recv_sem=rsem.at[phase],
            device_id=peer, device_id_type=MESH,
        ).start()

    def arrived(phase, like):
        pltpu.make_async_copy(like, like, rsem.at[phase]).wait()

    def sent(phase, like):
        pltpu.make_async_copy(like, like, ssem.at[phase]).wait()

    loads[0].wait()
    loads[1].wait()
    loads[2].wait()
    rp = split(r_v[...], 2)
    halves = []
    for h in range(2):
        rows = slice(128 * h, 128 * h + 128)
        b = m_v[rows, :].astype(f32) + (g_v[0, rows, :].astype(f32) + g_v[1, rows, :].astype(f32))
        bp = split(b, 2)
        bhi[rows, :] = bp[0]
        blo[rows, :] = bp[1]
        halves.append(dots(bp, rp, NT, 2) * 0.125)
    pc_send[...] = jnp.concatenate(halves, axis=1)

    pl.semaphore_wait(barrier, len(greeted))

    send(0, pc_send, pc_recv, mate)
    arrived(0, pc_recv)
    p_send[...] = (pc_send[...] + pc_recv[...]).reshape(16, 8, 128)
    p_recv[q] = p_send[q]
    for o, peer in plane:
        send(1, p_send.at[o], p_recv.at[q], peer)
    arrived(1, p_recv.at[pl.ds(0, 15)])
    mine = p_recv[0]
    for k in range(1, 16):
        mine = mine + p_recv[k]
    pk[q] = mine
    qk[z] = mine
    for o, peer in plane:
        send(2, pk.at[q], pk.at[q], peer)
    for o, peer in column:
        send(3, qk.at[z], qk.at[z], peer)

    arrived(2, pk.at[pl.ds(0, 15)])
    pt = pk[...].reshape(128, 128).T
    pt = jnp.concatenate([pt[:64], pt[64:]], axis=1)
    ptp = split(pt, 3)
    for c in range(4):
        cols = slice(256 * c, 256 * c + 256)
        part = dots(ptp, [bhi[:, cols], blo[:, cols]], NN, 3)
        for k in range(2):
            for h in range(2):
                rr[4 * c + 2 * k + h] = part[32 * h : 32 * h + 32, 128 * k : 128 * k + 128]
    for o, peer in column:
        send(4, rr.at[o], rr_recv.at[z], peer)
    rr_recv[z] = rr[z]
    for o, peer in replicas:
        send(5, rr.at[pl.ds(2 * o, 2)], d_recv.at[dp], peer)
    d_recv[dp] = rr[pl.ds(2 * dp, 2)]

    def share_gram(t, first, second, phase):
        tp = split(t, 3)
        g = dots(tp, tp, NT, 3)
        first[y] = jnp.concatenate([g[:32], g[32:]], axis=1)
        for o, peer in ys:
            send(phase, first.at[y], first.at[y], peer)

    def pass_gram(first, second, phase):
        arrived(phase, first.at[pl.ds(0, 3)])
        second[x] = (first[0] + first[1]) + (first[2] + first[3])
        for o, peer in xs:
            send(phase + 1, second.at[x], second.at[x], peer)

    def whole_gram(second, phase):
        arrived(phase + 1, second.at[pl.ds(0, 3)])
        g = (second[0] + second[1]) + (second[2] + second[3])
        return jnp.concatenate([g, pltpu.roll(g, 64, 1)], axis=0)

    lanes = lax.broadcasted_iota(jnp.int32, (64, 128), 1)
    ranks = lax.broadcasted_iota(jnp.int32, (64, 128), 0)

    arrived(3, qk.at[pl.ds(0, 15)])
    qt = qk[...].reshape(128, 128).T
    qt = jnp.concatenate([qt[:64], qt[64:]], axis=1)
    share_gram(qt, gy, gx, 6)
    pass_gram(gy, gx, 6)

    arrived(5, d_recv.at[pl.ds(0, 7)])
    total = d_recv[0]
    for k in range(1, 8):
        total = total + d_recv[k]
    total = total.reshape(64, 128)
    for k in range(16):
        sd[k] = total[4 * k : 4 * k + 4, :]
    for o, peer in column:
        send(10, sd.at[o], sd_recv.at[z], peer)
    sd_recv[z] = sd[z]

    g = whole_gram(gx, 6)
    aug[...] = jnp.where(lanes < 64, g, jnp.where(lanes == ranks + 64, 1.0, 0.0))
    eliminate(aug)
    first_inverse = aug[:, 64:]
    qt1 = dots(split(first_inverse, 3), split(qt, 3), NN, 3)
    share_gram(qt1, hy, hx, 8)

    arrived(4, rr_recv.at[pl.ds(0, 15)])
    total = rr_recv[0]
    for k in range(1, 16):
        total = total + rr_recv[k]
    rr_all[z] = total
    for o, peer in column:
        send(11, rr_all.at[z], rr_all.at[z], peer)

    arrived(10, sd_recv.at[pl.ds(0, 15)])
    total = sd_recv[0]
    for k in range(1, 16):
        total = total + sd_recv[k]
    s_sub[z] = total * 0.125
    for o, peer in column:
        send(12, s_sub.at[z], s_sub.at[z], peer)

    pass_gram(hy, hx, 8)
    g = whole_gram(hx, 8)
    aug[...] = jnp.where(lanes < 64, g, aug[...])
    eliminate(aug)
    inverse = split(aug[:, 64:], 3)
    leftt = dots(inverse, ptp, NN, 3)
    lp = split(leftt, 2)
    l0 = lp[0].astype(f32)
    l1 = lp[1].astype(f32)
    left3 = jnp.concatenate([l0, l0, l1], axis=0).T.astype(bf16)

    arrived(12, s_sub.at[pl.ds(0, 15)])
    for k in range(16):
        s_all[dp, 4 * k : 4 * k + 4, :] = s_sub[k]
    for o, peer in replicas:
        send(13, s_all.at[dp], s_all.at[dp], peer)

    arrived(11, rr_all.at[pl.ds(0, 15)])
    for c in range(4):
        cols = slice(256 * c, 256 * c + 256)
        raw = jnp.concatenate(
            [jnp.concatenate([rr_all[4 * c + h], rr_all[4 * c + 2 + h]], axis=1) for h in range(2)], axis=0
        )
        right = dots(inverse, split(raw, 3), NN, 3)
        r0, r1 = split(right, 2)
        right3 = jnp.concatenate([r0, r1, r0], axis=0)
        projected = lax.dot_general(left3, right3, NN, preferred_element_type=f32)
        b = m_v[:, cols].astype(f32) + (g_v[0, :, cols].astype(f32) + g_v[1, :, cols].astype(f32))
        nm_v[:, cols] = (b - decay_part * projected).astype(bf16)
    nm_out = pltpu.make_async_copy(nm_v, nm_hbm.at[0], out_sem.at[0])
    nm_out.start()

    arrived(13, s_all.at[pl.ds(0, 7)])
    sums = None
    for k in range(8):
        shared = dots(inverse, split(s_all[k], 3), NN, 3)
        nr_v[:, 128 * k : 128 * k + 128] = shared
        sums = shared * shared if sums is None else sums + shared * shared
    sums = jnp.sum(sums, axis=1, keepdims=True)
    small = lax.broadcasted_iota(jnp.int32, (8, 128), 1)
    tile = jnp.zeros((8, 128), f32)
    for i in range(8):
        tile = jnp.where(small == i, jnp.broadcast_to(sums[8 * i : 8 * i + 8], (8, 128)), tile)
    sq[x] = tile
    for o, peer in xs:
        send(14, sq.at[x], sq.at[x], peer)
    arrived(14, sq.at[pl.ds(0, 3)])
    tile = (sq[0] + sq[1]) + (sq[2] + sq[3])
    tile = 1.0 / jnp.sqrt(tile + epsilon)
    factor = jnp.concatenate([lane_of(tile, i) for i in range(8)], axis=0)
    for k in range(8):
        nr_v[:, 128 * k : 128 * k + 128] = nr_v[:, 128 * k : 128 * k + 128] * factor
    nr_out = pltpu.make_async_copy(nr_v, nr_hbm, out_sem.at[1])
    nr_out.start()
    loads[3].wait()
    scale = learn_rate * math.sqrt(ROWS / COLS)
    for c in range(4):
        cols = slice(256 * c, 256 * c + 256)
        r0, r1 = split(nr_v[:, cols], 2)
        right3 = jnp.concatenate([r0, r1, r0], axis=0)
        step = lax.dot_general(left3, right3, NN, preferred_element_type=f32)
        nw_v[:, cols] = w_v[:, cols] - scale * step
    nw_out = pltpu.make_async_copy(nw_v, nw_hbm, out_sem.at[2])
    nw_out.start()

    sent(0, pc_send)
    sent(1, p_send.at[pl.ds(0, 15)])
    sent(2, pk.at[pl.ds(0, 15)])
    sent(3, qk.at[pl.ds(0, 15)])
    sent(4, rr.at[pl.ds(0, 15)])
    sent(5, d_recv.at[pl.ds(0, 7)])
    sent(6, gy.at[pl.ds(0, 3)])
    sent(7, gx.at[pl.ds(0, 3)])
    sent(8, hy.at[pl.ds(0, 3)])
    sent(9, hx.at[pl.ds(0, 3)])
    sent(10, sd.at[pl.ds(0, 15)])
    sent(11, rr_all.at[pl.ds(0, 15)])
    sent(12, s_sub.at[pl.ds(0, 15)])
    sent(13, s_all.at[pl.ds(0, 7)])
    sent(14, sq.at[pl.ds(0, 3)])
    nm_out.wait()
    nr_out.wait()
    nw_out.wait()


def local(weight, momentum, grads, right_factor):
    rows, cols = weight.shape
    rank = right_factor.shape[0]
    vm = pltpu.VMEM
    return pl.pallas_call(
        kernel,
        out_shape=(
            jax.ShapeDtypeStruct(weight.shape, f32),
            jax.ShapeDtypeStruct(momentum.shape, bf16),
            jax.ShapeDtypeStruct(right_factor.shape, f32),
        ),
        in_specs=[pl.BlockSpec(memory_space=pl.ANY)] * 4,
        out_specs=[pl.BlockSpec(memory_space=pl.ANY)] * 3,
        scratch_shapes=[
            vm((rows, cols), f32),
            vm((rows, cols), bf16),
            vm((2, rows, cols), bf16),
            vm((rank, cols), f32),
            vm((rows, cols), bf16),
            vm((rows, cols), bf16),
            vm((128, 128), f32),
            vm((128, 128), f32),
            vm((16, 8, 128), f32),
            vm((16, 8, 128), f32),
            vm((16, 8, 128), f32),
            vm((16, 8, 128), f32),
            vm((16, 32, 128), f32),
            vm((16, 32, 128), f32),
            vm((16, 32, 128), f32),
            vm((8, 2, 32, 128), f32),
            vm((16, 4, 128), f32),
            vm((16, 4, 128), f32),
            vm((16, 4, 128), f32),
            vm((8, 64, 128), f32),
            vm((4, 32, 128), f32),
            vm((4, 32, 128), f32),
            vm((4, 32, 128), f32),
            vm((4, 32, 128), f32),
            vm((64, 128), f32),
            vm((4, 8, 128), f32),
            vm((rows, cols), f32),
            vm((rows, cols), bf16),
            vm((rank, cols), f32),
            pltpu.SemaphoreType.DMA((4,)),
            pltpu.SemaphoreType.DMA((3,)),
            pltpu.SemaphoreType.DMA((15,)),
            pltpu.SemaphoreType.DMA((15,)),
        ],
        compiler_params=pltpu.CompilerParams(
            collective_id=0, has_side_effects=True, vmem_limit_bytes=48 * 1024 * 1024
        ),
        name="dion_step",
    )(weight, momentum, grads, right_factor)


def solution(mesh):
    placed = (
        P("fsdp", "tensor"),
        P("dp", "fsdp", "tensor"),
        P("dp", None, "fsdp", "tensor"),
        P(None, "tensor"),
    )
    return jax.shard_map(
        local,
        mesh=mesh,
        in_specs=placed,
        out_specs=(P("fsdp", "tensor"), P("dp", "fsdp", "tensor"), P(None, "tensor")),
        check_vma=False,
    )
```

```python
import functools
import math

import jax
import jax.numpy as jnp
from jax import lax
from jax.experimental import pallas as pl
from jax.experimental.pallas import tpu as pltpu
from jax.sharding import PartitionSpec as P

ROWS = 4096
COLS = 4096

decay_part = 0.05
learn_rate = 0.02
epsilon = 1e-06

MESH = pl.DeviceIdType.MESH
f32 = jnp.float32
bf16 = jnp.bfloat16
NN = (((1,), (0,)), ((), ()))
NT = (((1,), (1,)), ((), ()))

AWAY = (0, 3, -3, 6, -6)


def split(x, n):
    parts = []
    for k in range(n):
        part = x.astype(bf16)
        parts.append(part)
        if k < n - 1:
            x = x - part.astype(f32)
    return parts


def dots(a, b, dims, order):
    total = None
    pairs = [(i, j) for i in range(len(a)) for j in range(len(b)) if i + j < order]
    for i, j in sorted(pairs, key=lambda t: -(t[0] + t[1])):
        term = lax.dot_general(a[i], b[j], dims, preferred_element_type=f32)
        total = term if total is None else total + term
    return total


def row_of(v, j):
    return jnp.broadcast_to(v[j : j + 1, :], (8, 128))


def lane_of(v, j):
    return jnp.broadcast_to(v[:, j : j + 1], (8, 128))


def eliminate(ref):
    sub = lax.broadcasted_iota(jnp.int32, (8, 128), 0)

    def body(kb, _):
        o = pl.multiple_of(kb * 8, 8)
        shift = lax.rem(128 - 8 * kb, 128)
        R = ref[pl.ds(o, 8), :]
        W = [R] + [ref[8 * i : 8 * i + 8, :] for i in range(1, 8)]
        D = [pltpu.roll(w, shift, 1) for w in W]
        C = [[lane_of(d, j) for j in range(8)] for d in D]
        Ls = [[None] * 8 for _ in range(8)]
        us = []
        for j in range(8):
            r = lax.rsqrt(row_of(C[0][j], j))
            for i in range(8):
                Ls[i][j] = C[i][j] * r
            u = row_of(R, j) * r
            us.append(u)
            R = R - Ls[0][j] * u
            for k in range(j + 1, 8):
                s = row_of(Ls[0][j], k)
                for i in range(8):
                    C[i][k] = C[i][k] - Ls[i][j] * s
        U = us[0]
        for j in range(1, 8):
            U = jnp.where(sub == j, us[j], U)
        for i in range(1, 8):
            w = W[i]
            for j in range(8):
                w = w - Ls[i][j] * us[j]
            ref[8 * i : 8 * i + 8, :] = jnp.where(i > kb, w, W[i])
        ref[pl.ds(o, 8), :] = U
        return 0

    lax.fori_loop(0, 8, body, 0)


def kernel(
    w_hbm, m_hbm, g_hbm, r_hbm, nw_hbm, nm_hbm, nr_hbm,
    w_v, m_v, g_v, r_v, bhi, blo,
    pc_send, pc_recv, p_send, p_recv, pk, qk,
    rr, near, agg, far, rr_all, d_recv, sd, sd_recv, s_sub, s_all,
    gy, gx, hy, hx, aug, sq,
    nw_v, nm_v, nr_v,
    in_sem, out_sem, ssem, rsem,
):
    dp = lax.axis_index("dp")
    z = lax.axis_index("fsdp")
    x = lax.axis_index("tensor")
    y = dp // 2
    core = lax.rem(dp, 2)
    q = y * 4 + x

    loads = [
        pltpu.make_async_copy(m_hbm.at[0], m_v, in_sem.at[0]),
        pltpu.make_async_copy(g_hbm.at[0], g_v, in_sem.at[1]),
        pltpu.make_async_copy(r_hbm, r_v, in_sem.at[2]),
        pltpu.make_async_copy(w_hbm, w_v, in_sem.at[3]),
    ]
    for load in loads:
        load.start()

    def around(k):
        return lax.rem(z + k + 16, 16)

    mate = {"dp": y * 2 + 1 - core}
    across = [mate]
    for d in range(1, 16):
        o = lax.rem(q + d, 16)
        across.append({"dp": (o // 4) * 2 + 1 - core, "tensor": lax.rem(o, 4)})
    plane = []
    for d in range(1, 16):
        o = lax.rem(q + d, 16)
        plane.append((o, {"dp": (o // 4) * 2 + core, "tensor": lax.rem(o, 4)}))
    column = []
    for d in range(1, 16):
        o = lax.rem(z + d, 16)
        column.append((o, {"fsdp": o}))
    replicas = []
    for d in range(1, 8):
        o = lax.rem(dp + d, 8)
        replicas.append((o, {"dp": o}))
    ys, xs = [], []
    for d in range(1, 4):
        o = lax.rem(y + d, 4)
        ys.append((o, {"dp": o * 2 + core}))
        o = lax.rem(x + d, 4)
        xs.append((o, {"tensor": o}))

    barrier = pltpu.get_barrier_semaphore()
    everyone = [p for _, p in plane] + across
    greeted = [p for _, p in column] + everyone
    for p in greeted:
        pl.semaphore_signal(barrier, inc=1, device_id=p, device_id_type=MESH)

    def send(phase, src, dst, peer):
        pltpu.make_async_remote_copy(
            src_ref=src, dst_ref=dst, send_sem=ssem.at[phase], recv_sem=rsem.at[phase],
            device_id=peer, device_id_type=MESH,
        ).start()

    def arrived(phase, like):
        pltpu.make_async_copy(like, like, rsem.at[phase]).wait()

    def sent(phase, like):
        pltpu.make_async_copy(like, like, ssem.at[phase]).wait()

    loads[0].wait()
    loads[1].wait()
    loads[2].wait()
    rp = split(r_v[...], 2)
    halves = []
    for h in range(2):
        rows = slice(128 * h, 128 * h + 128)
        b = m_v[rows, :].astype(f32) + (g_v[0, rows, :].astype(f32) + g_v[1, rows, :].astype(f32))
        bp = split(b, 2)
        bhi[rows, :] = bp[0]
        blo[rows, :] = bp[1]
        halves.append(dots(bp, rp, NT, 2) * 0.125)
    pc_send[...] = jnp.concatenate(halves, axis=1)

    pl.semaphore_wait(barrier, len(greeted))

    send(0, pc_send, pc_recv, mate)
    arrived(0, pc_recv)
    p_send[...] = (pc_send[...] + pc_recv[...]).reshape(16, 8, 128)
    p_recv[q] = p_send[q]
    for o, peer in plane:
        send(1, p_send.at[o], p_recv.at[q], peer)
    arrived(1, p_recv.at[pl.ds(0, 15)])
    mine = p_recv[0]
    for k in range(1, 16):
        mine = mine + p_recv[k]
    pk[q] = mine
    qk[z] = mine
    for o, peer in plane:
        send(2, pk.at[q], pk.at[q], peer)
    for o, peer in column:
        send(3, qk.at[z], qk.at[z], peer)

    arrived(2, pk.at[pl.ds(0, 15)])
    pt = pk[...].reshape(128, 128).T
    pt = jnp.concatenate([pt[:64], pt[64:]], axis=1)
    ptp = split(pt, 3)
    for c in range(4):
        cols = slice(256 * c, 256 * c + 256)
        part = dots(ptp, [bhi[:, cols], blo[:, cols]], NN, 3)
        for k in range(2):
            for h in range(2):
                rr[4 * c + 2 * k + h] = part[32 * h : 32 * h + 32, 128 * k : 128 * k + 128]
    for k in (3, 4, 1, 2, 0):
        for side, step in enumerate((1, -1)):
            o = around(step + AWAY[k])
            send(4 if k > 2 else 15, rr.at[o], near.at[k, side], {"fsdp": around(step)})
    send(16, rr.at[around(8)], far.at[0], {"fsdp": around(8)})
    for o, peer in replicas:
        send(5, rr.at[pl.ds(2 * o, 2)], d_recv.at[dp], peer)
    d_recv[dp] = rr[pl.ds(2 * dp, 2)]

    def share_gram(t, first, second, phase):
        tp = split(t, 3)
        g = dots(tp, tp, NT, 3)
        first[y] = jnp.concatenate([g[:32], g[32:]], axis=1)
        for o, peer in ys:
            send(phase, first.at[y], first.at[y], peer)

    def pass_gram(first, second, phase):
        arrived(phase, first.at[pl.ds(0, 3)])
        second[x] = (first[0] + first[1]) + (first[2] + first[3])
        for o, peer in xs:
            send(phase + 1, second.at[x], second.at[x], peer)

    def whole_gram(second, phase):
        arrived(phase + 1, second.at[pl.ds(0, 3)])
        g = (second[0] + second[1]) + (second[2] + second[3])
        return jnp.concatenate([g, pltpu.roll(g, 64, 1)], axis=0)

    lanes = lax.broadcasted_iota(jnp.int32, (64, 128), 1)
    ranks = lax.broadcasted_iota(jnp.int32, (64, 128), 0)

    arrived(3, qk.at[pl.ds(0, 15)])
    qt = qk[...].reshape(128, 128).T
    qt = jnp.concatenate([qt[:64], qt[64:]], axis=1)
    share_gram(qt, gy, gx, 6)

    def forward(k):
        agg[k - 1] = rr[around(AWAY[k])] + near[k, 0] + near[k, 1]
        send(16, agg.at[k - 1], far.at[k], {"fsdp": around(AWAY[k])})

    arrived(4, near.at[pl.ds(3, 2)])
    forward(3)
    forward(4)
    arrived(15, near.at[pl.ds(0, 3)])
    forward(1)
    forward(2)
    pass_gram(gy, gx, 6)

    arrived(5, d_recv.at[pl.ds(0, 7)])
    total = d_recv[0]
    for k in range(1, 8):
        total = total + d_recv[k]
    total = total.reshape(64, 128)
    for k in range(16):
        sd[k] = total[4 * k : 4 * k + 4, :]
    for o, peer in column:
        send(10, sd.at[o], sd_recv.at[z], peer)
    sd_recv[z] = sd[z]

    g = whole_gram(gx, 6)
    aug[...] = jnp.where(lanes < 64, g, jnp.where(lanes == ranks + 64, 1.0, 0.0))
    eliminate(aug)
    first_inverse = aug[:, 64:]
    qt1 = dots(split(first_inverse, 3), split(qt, 3), NN, 3)
    share_gram(qt1, hy, hx, 8)

    total = rr[z] + near[0, 0] + near[0, 1]
    arrived(16, far)
    for k in range(5):
        total = total + far[k]
    rr_all[z] = total
    for k in (3, 4, 1, 2):
        send(16 + k, rr_all.at[z], rr_all.at[z], {"fsdp": around(AWAY[k])})
    for step in (8, 1, -1):
        send(11, rr_all.at[z], rr_all.at[z], {"fsdp": around(step)})

    arrived(10, sd_recv.at[pl.ds(0, 15)])
    total = sd_recv[0]
    for k in range(1, 16):
        total = total + sd_recv[k]
    s_sub[z] = total * 0.125
    for o, peer in column:
        send(12, s_sub.at[z], s_sub.at[z], peer)

    def hand_on(k):
        o = around(-AWAY[k])
        arrived(16 + k, rr_all.at[o])
        for step in (1, -1):
            send(11, rr_all.at[o], rr_all.at[o], {"fsdp": around(step)})

    pass_gram(hy, hx, 8)
    hand_on(1)
    hand_on(2)
    hand_on(3)
    hand_on(4)
    g = whole_gram(hx, 8)
    aug[...] = jnp.where(lanes < 64, g, aug[...])
    eliminate(aug)
    inverse = split(aug[:, 64:], 3)

    arrived(12, s_sub.at[pl.ds(0, 15)])
    for k in range(16):
        s_all[dp, 4 * k : 4 * k + 4, :] = s_sub[k]
    for o, peer in replicas:
        send(13, s_all.at[dp], s_all.at[dp], peer)
    shared = dots(inverse, split(s_all[dp], 3), NN, 3)
    sums = jnp.sum(shared * shared, axis=1, keepdims=True)
    small = lax.broadcasted_iota(jnp.int32, (8, 128), 1)
    tile = jnp.zeros((8, 128), f32)
    for i in range(8):
        tile = jnp.where(small == i, jnp.broadcast_to(sums[8 * i : 8 * i + 8], (8, 128)), tile)
    spot = core * 16 + q
    sq[spot] = tile
    for peer in everyone:
        send(14, sq.at[spot], sq.at[spot], peer)

    leftt = dots(inverse, ptp, NN, 3)
    lp = split(leftt, 2)
    l0 = lp[0].astype(f32)
    l1 = lp[1].astype(f32)
    left3 = jnp.concatenate([l0, l0, l1], axis=0).T.astype(bf16)

    arrived(11, rr_all.at[pl.ds(0, 11)])
    for c in range(4):
        cols = slice(256 * c, 256 * c + 256)
        raw = jnp.concatenate(
            [jnp.concatenate([rr_all[4 * c + h], rr_all[4 * c + 2 + h]], axis=1) for h in range(2)], axis=0
        )
        right = dots(inverse, split(raw, 3), NN, 3)
        r0, r1 = split(right, 2)
        right3 = jnp.concatenate([r0, r1, r0], axis=0)
        projected = lax.dot_general(left3, right3, NN, preferred_element_type=f32)
        b = m_v[:, cols].astype(f32) + (g_v[0, :, cols].astype(f32) + g_v[1, :, cols].astype(f32))
        nm_v[:, cols] = (b - decay_part * projected).astype(bf16)
    nm_out = pltpu.make_async_copy(nm_v, nm_hbm.at[0], out_sem.at[0])
    nm_out.start()

    arrived(13, s_all.at[pl.ds(0, 7)])
    for k in range(8):
        nr_v[:, 128 * k : 128 * k + 128] = dots(inverse, split(s_all[k], 3), NN, 3)
    arrived(14, sq.at[pl.ds(0, 31)])
    tile = sq[0]
    for k in range(1, 32):
        tile = tile + sq[k]
    tile = 1.0 / jnp.sqrt(tile + epsilon)
    factor = jnp.concatenate([lane_of(tile, i) for i in range(8)], axis=0)
    for k in range(8):
        nr_v[:, 128 * k : 128 * k + 128] = nr_v[:, 128 * k : 128 * k + 128] * factor
    nr_out = pltpu.make_async_copy(nr_v, nr_hbm, out_sem.at[1])
    nr_out.start()
    loads[3].wait()
    scale = learn_rate * math.sqrt(ROWS / COLS)
    for c in range(4):
        cols = slice(256 * c, 256 * c + 256)
        r0, r1 = split(nr_v[:, cols], 2)
        right3 = jnp.concatenate([r0, r1, r0], axis=0)
        step = lax.dot_general(left3, right3, NN, preferred_element_type=f32)
        nw_v[:, cols] = w_v[:, cols] - scale * step
    nw_out = pltpu.make_async_copy(nw_v, nw_hbm, out_sem.at[2])
    nw_out.start()

    sent(0, pc_send)
    sent(1, p_send.at[pl.ds(0, 15)])
    sent(2, pk.at[pl.ds(0, 15)])
    sent(3, qk.at[pl.ds(0, 15)])
    sent(4, rr.at[pl.ds(0, 4)])
    sent(15, rr.at[pl.ds(0, 6)])
    sent(16, far)
    for k in range(1, 5):
        sent(16 + k, rr_all.at[0])
    sent(5, d_recv.at[pl.ds(0, 7)])
    sent(6, gy.at[pl.ds(0, 3)])
    sent(7, gx.at[pl.ds(0, 3)])
    sent(8, hy.at[pl.ds(0, 3)])
    sent(9, hx.at[pl.ds(0, 3)])
    sent(10, sd.at[pl.ds(0, 15)])
    sent(11, rr_all.at[pl.ds(0, 11)])
    sent(12, s_sub.at[pl.ds(0, 15)])
    sent(13, s_all.at[pl.ds(0, 7)])
    sent(14, sq.at[pl.ds(0, 31)])
    nm_out.wait()
    nr_out.wait()
    nw_out.wait()


def place(a, b, c, x, y, z, u, v, w, isem, osem):
    there = [(a, u, x), (b, v, y), (c, w, z)]
    reads = [pltpu.make_async_copy(s, m, isem.at[k]) for k, (s, m, t) in enumerate(there)]
    writes = [pltpu.make_async_copy(m, t, osem.at[k]) for k, (s, m, t) in enumerate(there)]
    for k in (2, 1, 0):
        reads[k].start()
    for k in (2, 1, 0):
        reads[k].wait()
        writes[k].start()
    for k in (2, 1, 0):
        writes[k].wait()


def local(weight, momentum, grads, right_factor):
    rows, cols = weight.shape
    rank = right_factor.shape[0]
    vm = pltpu.VMEM
    results = (
        jax.ShapeDtypeStruct(weight.shape, f32),
        jax.ShapeDtypeStruct(momentum.shape, bf16),
        jax.ShapeDtypeStruct(right_factor.shape, f32),
    )
    made = pl.pallas_call(
        kernel,
        out_shape=results,
        in_specs=[pl.BlockSpec(memory_space=pltpu.HBM)] * 4,
        out_specs=[pl.BlockSpec(memory_space=pl.ANY)] * 3,
        scratch_shapes=[
            vm((rows, cols), f32),
            vm((rows, cols), bf16),
            vm((2, rows, cols), bf16),
            vm((rank, cols), f32),
            vm((rows, cols), bf16),
            vm((rows, cols), bf16),
            vm((128, 128), f32),
            vm((128, 128), f32),
            vm((16, 8, 128), f32),
            vm((16, 8, 128), f32),
            vm((16, 8, 128), f32),
            vm((16, 8, 128), f32),
            vm((16, 32, 128), f32),
            vm((5, 2, 32, 128), f32),
            vm((4, 32, 128), f32),
            vm((5, 32, 128), f32),
            vm((16, 32, 128), f32),
            vm((8, 2, 32, 128), f32),
            vm((16, 4, 128), f32),
            vm((16, 4, 128), f32),
            vm((16, 4, 128), f32),
            vm((8, 64, 128), f32),
            vm((4, 32, 128), f32),
            vm((4, 32, 128), f32),
            vm((4, 32, 128), f32),
            vm((4, 32, 128), f32),
            vm((64, 128), f32),
            vm((32, 8, 128), f32),
            vm((rows, cols), f32),
            vm((rows, cols), bf16),
            vm((rank, cols), f32),
            pltpu.SemaphoreType.DMA((4,)),
            pltpu.SemaphoreType.DMA((3,)),
            pltpu.SemaphoreType.DMA((21,)),
            pltpu.SemaphoreType.DMA((21,)),
        ],
        compiler_params=pltpu.CompilerParams(
            collective_id=0, has_side_effects=True, vmem_limit_bytes=63 * 1024 * 1024
        ),
        name="dion_step",
    )(weight, momentum, grads, right_factor)
    return pl.pallas_call(
        place,
        out_shape=results,
        in_specs=[pl.BlockSpec(memory_space=pl.ANY)] * 3,
        out_specs=[pl.BlockSpec(memory_space=pl.ANY)] * 3,
        scratch_shapes=[vm(r.shape, r.dtype) for r in results]
        + [pltpu.SemaphoreType.DMA((3,)), pltpu.SemaphoreType.DMA((3,))],
        name="place",
    )(*made)


def solution(mesh):
    placed = (
        P("fsdp", "tensor"),
        P("dp", "fsdp", "tensor"),
        P("dp", None, "fsdp", "tensor"),
        P(None, "tensor"),
    )
    return jax.shard_map(
        local,
        mesh=mesh,
        in_specs=placed,
        out_specs=(P("fsdp", "tensor"), P("dp", "fsdp", "tensor"), P(None, "tensor")),
        check_vma=False,
    )
```

```python
import functools
import math

import jax
import jax.numpy as jnp
from jax import lax
from jax.experimental import pallas as pl
from jax.experimental.pallas import tpu as pltpu
from jax.sharding import PartitionSpec as P

ROWS = 4096
COLS = 4096

decay_part = 0.05
learn_rate = 0.02
epsilon = 1e-06

MESH = pl.DeviceIdType.MESH
f32 = jnp.float32
bf16 = jnp.bfloat16
NN = (((1,), (0,)), ((), ()))
NT = (((1,), (1,)), ((), ()))

AWAY = (0, 3, -3, 6, -6)


def split(x, n):
    parts = []
    for k in range(n):
        part = x.astype(bf16)
        parts.append(part)
        if k < n - 1:
            x = x - part.astype(f32)
    return parts


def dots(a, b, dims, order):
    total = None
    pairs = [(i, j) for i in range(len(a)) for j in range(len(b)) if i + j < order]
    for i, j in sorted(pairs, key=lambda t: -(t[0] + t[1])):
        term = lax.dot_general(a[i], b[j], dims, preferred_element_type=f32)
        total = term if total is None else total + term
    return total


def row_of(v, j):
    return jnp.broadcast_to(v[j : j + 1, :], (8, 128))


def lane_of(v, j):
    return jnp.broadcast_to(v[:, j : j + 1], (8, 128))


def eliminate(ref):
    sub = lax.broadcasted_iota(jnp.int32, (8, 128), 0)

    def body(kb, _):
        o = pl.multiple_of(kb * 8, 8)
        shift = lax.rem(128 - 8 * kb, 128)
        R = ref[pl.ds(o, 8), :]
        W = [R] + [ref[8 * i : 8 * i + 8, :] for i in range(1, 8)]
        D = [pltpu.roll(w, shift, 1) for w in W]
        C = [[lane_of(d, j) for j in range(8)] for d in D]
        Ls = [[None] * 8 for _ in range(8)]
        us = []
        for j in range(8):
            r = lax.rsqrt(row_of(C[0][j], j))
            for i in range(8):
                Ls[i][j] = C[i][j] * r
            u = row_of(R, j) * r
            us.append(u)
            R = R - Ls[0][j] * u
            for k in range(j + 1, 8):
                s = row_of(Ls[0][j], k)
                for i in range(8):
                    C[i][k] = C[i][k] - Ls[i][j] * s
        U = us[0]
        for j in range(1, 8):
            U = jnp.where(sub == j, us[j], U)
        for i in range(1, 8):
            w = W[i]
            for j in range(8):
                w = w - Ls[i][j] * us[j]
            ref[8 * i : 8 * i + 8, :] = jnp.where(i > kb, w, W[i])
        ref[pl.ds(o, 8), :] = U
        return 0

    lax.fori_loop(0, 8, body, 0)


def kernel(
    m_hbm, g_hbm, r_hbm, left_hbm, nm_hbm, nr_hbm,
    m_v, g_v, r_v, bhi, blo,
    p_send, p_recv, pk, qk,
    rr, near, agg, far, rr_all, d_recv, sd, sd_recv, s_sub, s_all,
    gy, gx, hy, hx, aug, sq,
    left_v, nm_v, nr_v,
    in_sem, out_sem, ssem, rsem, beyond,
):
    dp = lax.axis_index("dp")
    z = lax.axis_index("fsdp")
    x = lax.axis_index("tensor")
    y = dp // 2
    core = lax.rem(dp, 2)
    q = y * 4 + x

    loads = [
        pltpu.make_async_copy(m_hbm.at[0], m_v, in_sem.at[0]),
        pltpu.make_async_copy(g_hbm.at[0], g_v, in_sem.at[1]),
        pltpu.make_async_copy(r_hbm, r_v, in_sem.at[2]),
    ]
    for load in loads:
        load.start()

    def around(k):
        return lax.rem(z + k + 16, 16)

    across = []
    for d in range(16):
        o = lax.rem(q + d, 16)
        across.append((o, {"dp": (o // 4) * 2 + 1 - core, "tensor": lax.rem(o, 4)}))
    plane = []
    for d in range(1, 16):
        o = lax.rem(q + d, 16)
        plane.append((o, {"dp": (o // 4) * 2 + core, "tensor": lax.rem(o, 4)}))
    column = []
    for d in range(1, 16):
        o = lax.rem(z + d, 16)
        column.append((o, {"fsdp": o}))
    replicas = []
    for d in range(1, 8):
        o = lax.rem(dp + d, 8)
        replicas.append((o, {"dp": o}))
    ys, xs = [], []
    for d in range(1, 4):
        o = lax.rem(y + d, 4)
        ys.append((o, {"dp": o * 2 + core}))
        o = lax.rem(x + d, 4)
        xs.append((o, {"tensor": o}))

    barrier = pltpu.get_barrier_semaphore()
    everyone = plane + across
    greeted = [p for _, p in everyone] + [{"fsdp": around(k)} for d in range(1, 5) for k in (d, -d)]
    for p in greeted:
        pl.semaphore_signal(barrier, inc=1, device_id=p, device_id_type=MESH)

    def send(phase, src, dst, peer):
        pltpu.make_async_remote_copy(
            src_ref=src, dst_ref=dst, send_sem=ssem.at[phase], recv_sem=rsem.at[phase],
            device_id=peer, device_id_type=MESH,
        ).start()

    def arrived(phase, like):
        pltpu.make_async_copy(like, like, rsem.at[phase]).wait()

    def sent(phase, like):
        pltpu.make_async_copy(like, like, ssem.at[phase]).wait()

    loads[0].wait()
    loads[1].wait()
    loads[2].wait()
    rp = split(r_v[...], 2)
    halves = []
    for h in range(2):
        rows = slice(128 * h, 128 * h + 128)
        b = m_v[rows, :].astype(f32) + (g_v[0, rows, :].astype(f32) + g_v[1, rows, :].astype(f32))
        bp = split(b, 2)
        bhi[rows, :] = bp[0]
        blo[rows, :] = bp[1]
        halves.append(dots(bp, rp, NT, 2) * 0.125)
    p_send[...] = jnp.concatenate(halves, axis=1).reshape(16, 8, 128)

    pl.semaphore_wait(barrier, len(greeted))
    for k in (4, -4):
        pl.semaphore_signal(beyond, inc=1, device_id={"fsdp": around(k)}, device_id_type=MESH)

    spot = core * 16 + q
    for o, peer in everyone:
        send(1, p_send.at[o], p_recv.at[spot], peer)
    p_recv[spot] = p_send[q]
    pl.semaphore_wait(beyond, 2)
    arrived(1, p_recv.at[pl.ds(0, 31)])
    mine = p_recv[0]
    for k in range(1, 32):
        mine = mine + p_recv[k]
    pk[q] = mine
    qk[z] = mine
    for o, peer in plane:
        send(2, pk.at[q], pk.at[q], peer)
    for o, peer in column:
        send(3, qk.at[z], qk.at[z], peer)

    arrived(2, pk.at[pl.ds(0, 15)])
    pt = pk[...].reshape(128, 128).T
    pt = jnp.concatenate([pt[:64], pt[64:]], axis=1)
    ptp = split(pt, 3)
    for c in range(4):
        cols = slice(256 * c, 256 * c + 256)
        part = dots(ptp, [bhi[:, cols], blo[:, cols]], NN, 3)
        for k in range(2):
            for h in range(2):
                rr[4 * c + 2 * k + h] = part[32 * h : 32 * h + 32, 128 * k : 128 * k + 128]
    for k in (3, 4, 1, 2, 0):
        for side, step in enumerate((1, -1)):
            o = around(step + AWAY[k])
            send(4 if k > 2 else 15, rr.at[o], near.at[k, side], {"fsdp": around(step)})
    send(16, rr.at[around(8)], far.at[0], {"fsdp": around(8)})
    for o, peer in replicas:
        send(5, rr.at[pl.ds(2 * o, 2)], d_recv.at[dp], peer)
    d_recv[dp] = rr[pl.ds(2 * dp, 2)]

    def share_gram(t, first, second, phase):
        tp = split(t, 3)
        g = dots(tp, tp, NT, 3)
        first[y] = jnp.concatenate([g[:32], g[32:]], axis=1)
        for o, peer in ys:
            send(phase, first.at[y], first.at[y], peer)

    def pass_gram(first, second, phase):
        arrived(phase, first.at[pl.ds(0, 3)])
        second[x] = (first[0] + first[1]) + (first[2] + first[3])
        for o, peer in xs:
            send(phase + 1, second.at[x], second.at[x], peer)

    def whole_gram(second, phase):
        arrived(phase + 1, second.at[pl.ds(0, 3)])
        g = (second[0] + second[1]) + (second[2] + second[3])
        return jnp.concatenate([g, pltpu.roll(g, 64, 1)], axis=0)

    lanes = lax.broadcasted_iota(jnp.int32, (64, 128), 1)
    ranks = lax.broadcasted_iota(jnp.int32, (64, 128), 0)

    arrived(3, qk.at[pl.ds(0, 15)])
    qt = qk[...].reshape(128, 128).T
    qt = jnp.concatenate([qt[:64], qt[64:]], axis=1)
    share_gram(qt, gy, gx, 6)

    def forward(k):
        agg[k - 1] = rr[around(AWAY[k])] + near[k, 0] + near[k, 1]
        send(16, agg.at[k - 1], far.at[k], {"fsdp": around(AWAY[k])})

    arrived(4, near.at[pl.ds(3, 2)])
    forward(3)
    forward(4)
    arrived(15, near.at[pl.ds(0, 3)])
    forward(1)
    forward(2)
    pass_gram(gy, gx, 6)

    arrived(5, d_recv.at[pl.ds(0, 7)])
    total = d_recv[0]
    for k in range(1, 8):
        total = total + d_recv[k]
    total = total.reshape(64, 128)
    for k in range(16):
        sd[k] = total[4 * k : 4 * k + 4, :]
    for o, peer in column:
        send(10, sd.at[o], sd_recv.at[z], peer)
    sd_recv[z] = sd[z]

    g = whole_gram(gx, 6)
    aug[...] = jnp.where(lanes < 64, g, jnp.where(lanes == ranks + 64, 1.0, 0.0))
    eliminate(aug)
    first_inverse = aug[:, 64:]
    qt1 = dots(split(first_inverse, 3), split(qt, 3), NN, 3)
    share_gram(qt1, hy, hx, 8)

    total = rr[z] + near[0, 0] + near[0, 1]
    arrived(16, far)
    for k in range(5):
        total = total + far[k]
    rr_all[z] = total
    for k in (3, 4, 1, 2):
        send(16 + k, rr_all.at[z], rr_all.at[z], {"fsdp": around(AWAY[k])})
    for step in (8, 1, -1):
        send(11, rr_all.at[z], rr_all.at[z], {"fsdp": around(step)})

    arrived(10, sd_recv.at[pl.ds(0, 15)])
    total = sd_recv[0]
    for k in range(1, 16):
        total = total + sd_recv[k]
    s_sub[z] = total * 0.125
    for o, peer in column:
        send(12, s_sub.at[z], s_sub.at[z], peer)

    def hand_on(k):
        o = around(-AWAY[k])
        arrived(16 + k, rr_all.at[o])
        for step in (1, -1):
            send(11, rr_all.at[o], rr_all.at[o], {"fsdp": around(step)})

    pass_gram(hy, hx, 8)
    hand_on(1)
    hand_on(2)
    hand_on(3)
    hand_on(4)
    g = whole_gram(hx, 8)
    aug[...] = jnp.where(lanes < 64, g, aug[...])
    eliminate(aug)
    inverse = split(aug[:, 64:], 3)

    arrived(12, s_sub.at[pl.ds(0, 15)])
    for k in range(16):
        s_all[dp, 4 * k : 4 * k + 4, :] = s_sub[k]
    for o, peer in replicas:
        send(13, s_all.at[dp], s_all.at[dp], peer)
    shared = dots(inverse, split(s_all[dp], 3), NN, 3)
    sums = jnp.sum(shared * shared, axis=1, keepdims=True)
    small = lax.broadcasted_iota(jnp.int32, (8, 128), 1)
    tile = jnp.zeros((8, 128), f32)
    for i in range(8):
        tile = jnp.where(small == i, jnp.broadcast_to(sums[8 * i : 8 * i + 8], (8, 128)), tile)
    sq[spot] = tile
    for _, peer in everyone:
        send(14, sq.at[spot], sq.at[spot], peer)

    leftt = dots(inverse, ptp, NN, 3)
    lp = split(leftt, 2)
    l0 = lp[0].astype(f32)
    l1 = lp[1].astype(f32)
    left3 = jnp.concatenate([l0, l0, l1], axis=0).T.astype(bf16)
    left_v[...] = left3
    left_out = pltpu.make_async_copy(left_v, left_hbm, out_sem.at[2])
    left_out.start()

    arrived(11, rr_all.at[pl.ds(0, 11)])
    for c in range(4):
        cols = slice(256 * c, 256 * c + 256)
        raw = jnp.concatenate(
            [jnp.concatenate([rr_all[4 * c + h], rr_all[4 * c + 2 + h]], axis=1) for h in range(2)], axis=0
        )
        right = dots(inverse, split(raw, 3), NN, 3)
        r0, r1 = split(right, 2)
        right3 = jnp.concatenate([r0, r1, r0], axis=0)
        projected = lax.dot_general(left3, right3, NN, preferred_element_type=f32)
        b = m_v[:, cols].astype(f32) + (g_v[0, :, cols].astype(f32) + g_v[1, :, cols].astype(f32))
        nm_v[:, cols] = (b - decay_part * projected).astype(bf16)
    nm_out = pltpu.make_async_copy(nm_v, nm_hbm.at[0], out_sem.at[0])
    nm_out.start()

    arrived(13, s_all.at[pl.ds(0, 7)])
    for k in range(8):
        nr_v[:, 128 * k : 128 * k + 128] = dots(inverse, split(s_all[k], 3), NN, 3)
    arrived(14, sq.at[pl.ds(0, 31)])
    tile = sq[0]
    for k in range(1, 32):
        tile = tile + sq[k]
    tile = 1.0 / jnp.sqrt(tile + epsilon)
    factor = jnp.concatenate([lane_of(tile, i) for i in range(8)], axis=0)
    for k in range(8):
        nr_v[:, 128 * k : 128 * k + 128] = nr_v[:, 128 * k : 128 * k + 128] * factor
    nr_out = pltpu.make_async_copy(nr_v, nr_hbm, out_sem.at[1])
    nr_out.start()

    sent(1, p_recv.at[pl.ds(0, 31)])
    sent(2, pk.at[pl.ds(0, 15)])
    sent(3, qk.at[pl.ds(0, 15)])
    sent(4, rr.at[pl.ds(0, 4)])
    sent(15, rr.at[pl.ds(0, 6)])
    sent(16, far)
    for k in range(1, 5):
        sent(16 + k, rr_all.at[0])
    sent(5, d_recv.at[pl.ds(0, 7)])
    sent(6, gy.at[pl.ds(0, 3)])
    sent(7, gx.at[pl.ds(0, 3)])
    sent(8, hy.at[pl.ds(0, 3)])
    sent(9, hx.at[pl.ds(0, 3)])
    sent(10, sd.at[pl.ds(0, 15)])
    sent(11, rr_all.at[pl.ds(0, 11)])
    sent(12, s_sub.at[pl.ds(0, 15)])
    sent(13, s_all.at[pl.ds(0, 7)])
    sent(14, sq.at[pl.ds(0, 31)])
    nm_out.wait()
    nr_out.wait()
    left_out.wait()


def finish(
    w_hbm, left_hbm, nm_in, nr_in, nw_out, nm_out, nr_out,
    w_v, left_v, nm_v, nr_v, isem, osem,
):
    rows = w_v.shape[1]
    parts = range(w_v.shape[0])
    reads = [
        pltpu.make_async_copy(nr_in, nr_v, isem.at[0]),
        pltpu.make_async_copy(left_hbm, left_v, isem.at[1]),
    ]
    reads += [pltpu.make_async_copy(w_hbm.at[pl.ds(rows * k, rows)], w_v.at[k], isem.at[3 + k]) for k in parts]
    reads.append(pltpu.make_async_copy(nm_in, nm_v, isem.at[2]))
    for read in reads:
        read.start()
    reads[0].wait()
    writes = [pltpu.make_async_copy(nr_v, nr_out, osem.at[0])]
    writes[0].start()
    scale = learn_rate * math.sqrt(ROWS / COLS)
    r0, r1 = split(nr_v[...], 2)
    right3 = jnp.concatenate([r0, r1, r0], axis=0)
    reads[1].wait()
    for k in parts:
        reads[2 + k].wait()
        step = lax.dot_general(left_v[rows * k : rows * k + rows], right3, NN, preferred_element_type=f32)
        w_v[k] = w_v[k] - scale * step
        writes.append(pltpu.make_async_copy(w_v.at[k], nw_out.at[pl.ds(rows * k, rows)], osem.at[2 + k]))
        writes[-1].start()
    reads[-1].wait()
    writes.append(pltpu.make_async_copy(nm_v, nm_out, osem.at[1]))
    writes[-1].start()
    for write in writes:
        write.wait()


def local(weight, momentum, grads, right_factor):
    rows, cols = weight.shape
    rank = right_factor.shape[0]
    vm = pltpu.VMEM
    new_weight = jax.ShapeDtypeStruct(weight.shape, f32)
    new_momentum = jax.ShapeDtypeStruct(momentum.shape, bf16)
    new_right = jax.ShapeDtypeStruct(right_factor.shape, f32)
    left, made_momentum, made_right = pl.pallas_call(
        kernel,
        out_shape=(jax.ShapeDtypeStruct((rows, 3 * rank), bf16), new_momentum, new_right),
        in_specs=[pl.BlockSpec(memory_space=pltpu.HBM)] * 3,
        out_specs=[pl.BlockSpec(memory_space=pl.ANY)] * 3,
        scratch_shapes=[
            vm((rows, cols), bf16),
            vm((2, rows, cols), bf16),
            vm((rank, cols), f32),
            vm((rows, cols), bf16),
            vm((rows, cols), bf16),
            vm((16, 8, 128), f32),
            vm((32, 8, 128), f32),
            vm((16, 8, 128), f32),
            vm((16, 8, 128), f32),
            vm((16, 32, 128), f32),
            vm((5, 2, 32, 128), f32),
            vm((4, 32, 128), f32),
            vm((5, 32, 128), f32),
            vm((16, 32, 128), f32),
            vm((8, 2, 32, 128), f32),
            vm((16, 4, 128), f32),
            vm((16, 4, 128), f32),
            vm((16, 4, 128), f32),
            vm((8, 64, 128), f32),
            vm((4, 32, 128), f32),
            vm((4, 32, 128), f32),
            vm((4, 32, 128), f32),
            vm((4, 32, 128), f32),
            vm((64, 128), f32),
            vm((32, 8, 128), f32),
            vm((rows, 3 * rank), bf16),
            vm((rows, cols), bf16),
            vm((rank, cols), f32),
            pltpu.SemaphoreType.DMA((3,)),
            pltpu.SemaphoreType.DMA((3,)),
            pltpu.SemaphoreType.DMA((21,)),
            pltpu.SemaphoreType.DMA((21,)),
            pltpu.SemaphoreType.REGULAR,
        ],
        compiler_params=pltpu.CompilerParams(
            collective_id=0, has_side_effects=True, vmem_limit_bytes=63 * 1024 * 1024
        ),
        name="dion_step",
    )(momentum, grads, right_factor)
    parts = 4
    return pl.pallas_call(
        finish,
        out_shape=(new_weight, new_momentum, new_right),
        in_specs=[pl.BlockSpec(memory_space=pl.ANY)] * 4,
        out_specs=[pl.BlockSpec(memory_space=pl.ANY)] * 3,
        scratch_shapes=[
            vm((parts, rows // parts, cols), f32),
            vm((rows, 3 * rank), bf16),
            vm((1, rows, cols), bf16),
            vm((rank, cols), f32),
            pltpu.SemaphoreType.DMA((3 + parts,)),
            pltpu.SemaphoreType.DMA((2 + parts,)),
        ],
        compiler_params=pltpu.CompilerParams(vmem_limit_bytes=63 * 1024 * 1024),
        name="place",
    )(weight, left, made_momentum, made_right)


def solution(mesh):
    placed = (
        P("fsdp", "tensor"),
        P("dp", "fsdp", "tensor"),
        P("dp", None, "fsdp", "tensor"),
        P(None, "tensor"),
    )
    return jax.shard_map(
        local,
        mesh=mesh,
        in_specs=placed,
        out_specs=(P("fsdp", "tensor"), P("dp", "fsdp", "tensor"), P(None, "tensor")),
        check_vma=False,
    )
```

```python
import functools
import math

import jax
import jax.numpy as jnp
from jax import lax
from jax.experimental import pallas as pl
from jax.experimental.pallas import tpu as pltpu
from jax.sharding import PartitionSpec as P

ROWS = 4096
COLS = 4096

decay_part = 0.05
learn_rate = 0.02
epsilon = 1e-06

MESH = pl.DeviceIdType.MESH
f32 = jnp.float32
bf16 = jnp.bfloat16
NN = (((1,), (0,)), ((), ()))
NT = (((1,), (1,)), ((), ()))

AWAY = (0, 3, -3, 6, -6)


def split(x, n):
    parts = []
    for k in range(n):
        part = x.astype(bf16)
        parts.append(part)
        if k < n - 1:
            x = x - part.astype(f32)
    return parts


def dots(a, b, dims, order):
    total = None
    pairs = [(i, j) for i in range(len(a)) for j in range(len(b)) if i + j < order]
    for i, j in sorted(pairs, key=lambda t: -(t[0] + t[1])):
        term = lax.dot_general(a[i], b[j], dims, preferred_element_type=f32)
        total = term if total is None else total + term
    return total


def row_of(v, j):
    return jnp.broadcast_to(v[j : j + 1, :], (8, 128))


def lane_of(v, j):
    return jnp.broadcast_to(v[:, j : j + 1], (8, 128))


def eliminate(ref):
    sub = lax.broadcasted_iota(jnp.int32, (8, 128), 0)
    W = [ref[8 * i : 8 * i + 8, :] for i in range(8)]
    for kb in range(8):
        C = [[lane_of(w, 8 * kb + j) for j in range(8)] for w in W]
        Ls = [[None] * 8 for _ in W]
        R = W[0]
        us = []
        for j in range(8):
            r = lax.rsqrt(row_of(C[0][j], j))
            for i in range(len(W)):
                Ls[i][j] = C[i][j] * r
            u = row_of(R, j) * r
            us.append(u)
            R = R - Ls[0][j] * u
            for k in range(j + 1, 8):
                s = row_of(Ls[0][j], k)
                for i in range(len(W)):
                    C[i][k] = C[i][k] - Ls[i][j] * s
        U = us[0]
        for j in range(1, 8):
            U = jnp.where(sub == j, us[j], U)
        ref[8 * kb : 8 * kb + 8, :] = U
        rest = []
        for i in range(1, len(W)):
            w = W[i]
            for j in range(8):
                w = w - Ls[i][j] * us[j]
            rest.append(w)
        W = rest


def kernel(
    m_hbm, g_hbm, r_hbm, left_hbm, nm_hbm, nr_hbm,
    m_v, g_v, r_v, bhi, blo,
    p_send, p_recv, px, pk, qk,
    rr, near, agg, far, rr_all, d_recv, sd, sd_recv, s_sub, s_all,
    gy, gx, hy, hx, aug, sq,
    left_v, nm_v, nr_v,
    in_sem, out_sem, ssem, rsem, beyond,
):
    dp = lax.axis_index("dp")
    z = lax.axis_index("fsdp")
    x = lax.axis_index("tensor")
    y = dp // 2
    core = lax.bitwise_and(dp, 1)
    q = y * 4 + x

    def around(k):
        return lax.bitwise_and(z + (k + 16), 15)

    replicas = []
    for d in (4, 5, 2, 3, 6, 7, 1):
        o = lax.bitwise_xor(dp, d)
        replicas.append((o, {"dp": o}))
    ys, xs = [], []
    for d in (2, 1, 3):
        o = lax.bitwise_xor(y, d)
        ys.append((o, {"dp": o * 2 + core}))
        o = lax.bitwise_xor(x, d)
        xs.append((o, {"tensor": o}))

    barrier = pltpu.get_barrier_semaphore()
    greeted = [p for _, p in replicas] + [p for _, p in xs] + [{"fsdp": around(k)} for k in (2, -2, 1, -1)]
    for p in greeted:
        pl.semaphore_signal(barrier, inc=1, device_id=p, device_id_type=MESH)

    loads = [
        pltpu.make_async_copy(m_hbm.at[0], m_v, in_sem.at[0]),
        pltpu.make_async_copy(g_hbm.at[0], g_v, in_sem.at[1]),
        pltpu.make_async_copy(r_hbm, r_v, in_sem.at[2]),
    ]
    for load in loads:
        load.start()

    def tell(level, step):
        for k in (step, -step):
            pl.semaphore_signal(beyond.at[level], inc=1, device_id={"fsdp": around(k)}, device_id_type=MESH)

    def send(phase, src, dst, peer):
        pltpu.make_async_remote_copy(
            src_ref=src, dst_ref=dst, send_sem=ssem.at[phase], recv_sem=rsem.at[phase],
            device_id=peer, device_id_type=MESH,
        ).start()

    def arrived(phase, like):
        pltpu.make_async_copy(like, like, rsem.at[phase]).wait()

    def sent(phase, like):
        pltpu.make_async_copy(like, like, ssem.at[phase]).wait()

    loads[0].wait()
    loads[1].wait()
    loads[2].wait()
    rp = split(r_v[...], 2)
    halves = []
    for h in range(2):
        rows = slice(128 * h, 128 * h + 128)
        b = m_v[rows, :].astype(f32) + (g_v[0, rows, :].astype(f32) + g_v[1, rows, :].astype(f32))
        bp = split(b, 2)
        bhi[rows, :] = bp[0]
        blo[rows, :] = bp[1]
        halves.append(dots(bp, rp, NT, 2) * 0.125)
    p_send[...] = jnp.concatenate(halves, axis=1).reshape(4, 32, 128)

    pl.semaphore_wait(barrier, len(greeted))
    tell(0, 2)

    for o, peer in replicas:
        send(0, p_send.at[o // 2], p_recv.at[dp], peer)
    p_recv[dp] = p_send[y]
    pl.semaphore_wait(beyond.at[0], 2)
    tell(1, 4)
    arrived(0, p_recv.at[pl.ds(0, 7)])
    mine = p_recv[0]
    for k in range(1, 8):
        mine = mine + p_recv[k]
    px[x] = mine
    for o, peer in xs:
        send(1, px.at[x], px.at[x], peer)
    pl.semaphore_wait(beyond.at[1], 2)
    arrived(1, px.at[pl.ds(0, 3)])
    pk[y] = (px[0] + px[1]) + (px[2] + px[3])
    for o, peer in ys:
        send(2, pk.at[y], pk.at[y], peer)
    qk[z] = pk[y, pl.ds(pl.multiple_of(8 * x, 8), 8)]
    column = []
    for d in (8, 7, 9, 6, 10, 5, 11, 4, 12, 3, 13, 2, 14, 1, 15):
        o = around(d)
        column.append((o, {"fsdp": o}))
    for o, peer in column:
        send(3, qk.at[z], qk.at[z], peer)

    arrived(2, pk.at[pl.ds(0, 3)])
    pt = pk[...].reshape(128, 128).T
    pt = jnp.concatenate([pt[:64], pt[64:]], axis=1)
    ptp = split(pt, 3)
    for c in range(4):
        cols = slice(256 * c, 256 * c + 256)
        part = dots(ptp, [bhi[:, cols], blo[:, cols]], NN, 3)
        for k in range(2):
            for h in range(2):
                rr[4 * c + 2 * k + h] = part[32 * h : 32 * h + 32, 128 * k : 128 * k + 128]
    for o, peer in replicas:
        send(5, rr.at[pl.ds(2 * o, 2)], d_recv.at[dp], peer)
    for k in (3, 4, 1, 2, 0):
        for side, step in enumerate((1, -1)):
            o = around(step + AWAY[k])
            send(4 if k > 2 else 15, rr.at[o], near.at[k, side], {"fsdp": around(step)})
    send(16, rr.at[around(8)], far.at[0], {"fsdp": around(8)})
    d_recv[dp] = rr[pl.ds(2 * dp, 2)]

    def share_gram(t, first, second, phase):
        tp = split(t, 3)
        g = dots(tp, tp, NT, 3)
        first[y] = jnp.concatenate([g[:32], g[32:]], axis=1)
        for o, peer in ys:
            send(phase, first.at[y], first.at[y], peer)

    def pass_gram(first, second, phase):
        arrived(phase, first.at[pl.ds(0, 3)])
        second[x] = (first[0] + first[1]) + (first[2] + first[3])
        for o, peer in xs:
            send(phase + 1, second.at[x], second.at[x], peer)

    def whole_gram(second, phase):
        arrived(phase + 1, second.at[pl.ds(0, 3)])
        g = (second[0] + second[1]) + (second[2] + second[3])
        return jnp.concatenate([g, pltpu.roll(g, 64, 1)], axis=0)

    lanes = lax.broadcasted_iota(jnp.int32, (64, 128), 1)
    ranks = lax.broadcasted_iota(jnp.int32, (64, 128), 0)

    arrived(3, qk.at[pl.ds(0, 15)])
    qt = qk[...].reshape(128, 128).T
    qt = jnp.concatenate([qt[:64], qt[64:]], axis=1)
    share_gram(qt, gy, gx, 6)

    def forward(k):
        agg[k - 1] = rr[around(AWAY[k])] + near[k, 0] + near[k, 1]
        send(16, agg.at[k - 1], far.at[k], {"fsdp": around(AWAY[k])})

    pass_gram(gy, gx, 6)

    arrived(5, d_recv.at[pl.ds(0, 7)])
    total = d_recv[0]
    for k in range(1, 8):
        total = total + d_recv[k]
    total = total.reshape(64, 128)
    for k in range(16):
        sd[k] = total[4 * k : 4 * k + 4, :]
    for o, peer in column:
        send(10, sd.at[o], sd_recv.at[z], peer)
    sd_recv[z] = sd[z]
    arrived(4, near.at[pl.ds(3, 2)])
    forward(3)
    forward(4)
    arrived(15, near.at[pl.ds(0, 3)])
    forward(1)
    forward(2)

    g = whole_gram(gx, 6)
    aug[...] = jnp.where(lanes < 64, g, jnp.where(lanes == ranks + 64, 1.0, 0.0))
    eliminate(aug)
    first_inverse = aug[:, 64:]
    qt1 = dots(split(first_inverse, 3), split(qt, 3), NN, 3)
    share_gram(qt1, hy, hx, 8)

    arrived(10, sd_recv.at[pl.ds(0, 15)])
    total = sd_recv[0]
    for k in range(1, 16):
        total = total + sd_recv[k]
    s_sub[z] = total * 0.125
    for o, peer in column:
        send(12, s_sub.at[z], s_sub.at[z], peer)

    total = rr[z] + near[0, 0] + near[0, 1]
    arrived(16, far)
    for k in range(5):
        total = total + far[k]
    rr_all[z] = total
    for k in (3, 4, 1, 2):
        send(16 + k, rr_all.at[z], rr_all.at[z], {"fsdp": around(AWAY[k])})
    for step in (8, 1, -1):
        send(11, rr_all.at[z], rr_all.at[z], {"fsdp": around(step)})

    def hand_on(k):
        o = around(-AWAY[k])
        arrived(16 + k, rr_all.at[o])
        for step in (1, -1):
            send(11, rr_all.at[o], rr_all.at[o], {"fsdp": around(step)})

    pass_gram(hy, hx, 8)
    hand_on(1)
    hand_on(2)
    g = whole_gram(hx, 8)
    aug[...] = jnp.where(lanes < 64, g, aug[...])
    eliminate(aug)
    inverse = split(aug[:, 64:], 3)

    arrived(12, s_sub.at[pl.ds(0, 15)])
    for k in range(16):
        s_all[dp, 4 * k : 4 * k + 4, :] = s_sub[k]
    for o, peer in replicas:
        send(13, s_all.at[dp], s_all.at[dp], peer)
    shared = dots(inverse, split(s_all[dp], 3), NN, 3)
    sums = jnp.sum(shared * shared, axis=1, keepdims=True)
    small = lax.broadcasted_iota(jnp.int32, (8, 128), 1)
    tile = jnp.zeros((8, 128), f32)
    for i in range(8):
        tile = jnp.where(small == i, jnp.broadcast_to(sums[8 * i : 8 * i + 8], (8, 128)), tile)
    spot = core * 16 + q
    sq[spot] = tile
    everyone = []
    for d in (10, 9, 11, 6, 14, 2, 8, 5, 7, 13, 15, 1, 3, 4, 12, 0):
        o = lax.bitwise_xor(q, d)
        everyone.append({"dp": (o // 4) * 2 + 1 - core, "tensor": lax.bitwise_and(o, 3)})
        if d > 0:
            everyone.append({"dp": (o // 4) * 2 + core, "tensor": lax.bitwise_and(o, 3)})
    for peer in everyone:
        send(14, sq.at[spot], sq.at[spot], peer)

    hand_on(3)
    hand_on(4)
    leftt = dots(inverse, ptp, NN, 3)
    lp = split(leftt, 2)
    l0 = lp[0].astype(f32)
    l1 = lp[1].astype(f32)
    left3 = jnp.concatenate([l0, l0, l1], axis=0).T.astype(bf16)
    left_v[...] = left3
    left_out = pltpu.make_async_copy(left_v, left_hbm, out_sem.at[2])
    left_out.start()

    arrived(11, rr_all.at[pl.ds(0, 11)])
    for c in range(4):
        cols = slice(256 * c, 256 * c + 256)
        raw = jnp.concatenate(
            [jnp.concatenate([rr_all[4 * c + h], rr_all[4 * c + 2 + h]], axis=1) for h in range(2)], axis=0
        )
        right = dots(inverse, split(raw, 3), NN, 3)
        r0, r1 = split(right, 2)
        right3 = jnp.concatenate([r0, r1, r0], axis=0)
        projected = lax.dot_general(left3, right3, NN, preferred_element_type=f32)
        b = m_v[:, cols].astype(f32) + (g_v[0, :, cols].astype(f32) + g_v[1, :, cols].astype(f32))
        nm_v[:, cols] = (b - decay_part * projected).astype(bf16)
    nm_out = pltpu.make_async_copy(nm_v, nm_hbm.at[0], out_sem.at[0])
    nm_out.start()

    arrived(13, s_all.at[pl.ds(0, 7)])
    for k in range(8):
        nr_v[:, 128 * k : 128 * k + 128] = dots(inverse, split(s_all[k], 3), NN, 3)
    arrived(14, sq.at[pl.ds(0, 31)])
    tile = sq[0]
    for k in range(1, 32):
        tile = tile + sq[k]
    tile = 1.0 / jnp.sqrt(tile + epsilon)
    factor = jnp.concatenate([lane_of(tile, i) for i in range(8)], axis=0)
    for k in range(8):
        nr_v[:, 128 * k : 128 * k + 128] = nr_v[:, 128 * k : 128 * k + 128] * factor
    nr_out = pltpu.make_async_copy(nr_v, nr_hbm, out_sem.at[1])
    nr_out.start()

    sent(0, p_recv.at[pl.ds(0, 7)])
    sent(1, px.at[pl.ds(0, 3)])
    sent(2, pk.at[pl.ds(0, 3)])
    sent(3, qk.at[pl.ds(0, 15)])
    sent(4, rr.at[pl.ds(0, 4)])
    sent(15, rr.at[pl.ds(0, 6)])
    sent(16, far)
    for k in range(1, 5):
        sent(16 + k, rr_all.at[0])
    sent(5, d_recv.at[pl.ds(0, 7)])
    sent(6, gy.at[pl.ds(0, 3)])
    sent(7, gx.at[pl.ds(0, 3)])
    sent(8, hy.at[pl.ds(0, 3)])
    sent(9, hx.at[pl.ds(0, 3)])
    sent(10, sd.at[pl.ds(0, 15)])
    sent(11, rr_all.at[pl.ds(0, 11)])
    sent(12, s_sub.at[pl.ds(0, 15)])
    sent(13, s_all.at[pl.ds(0, 7)])
    sent(14, sq.at[pl.ds(0, 31)])
    nm_out.wait()
    nr_out.wait()
    left_out.wait()


def finish(
    w_hbm, left_hbm, nm_in, nr_in, nw_out, nm_out, nr_out,
    w_v, left_v, nm_v, nr_v, isem, osem,
):
    rows = w_v.shape[1]
    parts = range(w_v.shape[0])
    reads = [
        pltpu.make_async_copy(nr_in, nr_v, isem.at[0]),
        pltpu.make_async_copy(left_hbm, left_v, isem.at[1]),
    ]
    reads += [pltpu.make_async_copy(w_hbm.at[pl.ds(rows * k, rows)], w_v.at[k], isem.at[3 + k]) for k in parts]
    reads.append(pltpu.make_async_copy(nm_in, nm_v, isem.at[2]))
    for read in reads:
        read.start()
    reads[0].wait()
    writes = [pltpu.make_async_copy(nr_v, nr_out, osem.at[0])]
    writes[0].start()
    scale = learn_rate * math.sqrt(ROWS / COLS)
    r0, r1 = split(nr_v[...], 2)
    right3 = jnp.concatenate([r0, r1, r0], axis=0)
    reads[1].wait()
    for k in parts:
        reads[2 + k].wait()
        step = lax.dot_general(left_v[rows * k : rows * k + rows], right3, NN, preferred_element_type=f32)
        w_v[k] = w_v[k] - scale * step
        writes.append(pltpu.make_async_copy(w_v.at[k], nw_out.at[pl.ds(rows * k, rows)], osem.at[2 + k]))
        writes[-1].start()
    reads[-1].wait()
    writes.append(pltpu.make_async_copy(nm_v, nm_out, osem.at[1]))
    writes[-1].start()
    for write in writes:
        write.wait()


def local(weight, momentum, grads, right_factor):
    rows, cols = weight.shape
    rank = right_factor.shape[0]
    vm = pltpu.VMEM
    new_weight = jax.ShapeDtypeStruct(weight.shape, f32)
    new_momentum = jax.ShapeDtypeStruct(momentum.shape, bf16)
    new_right = jax.ShapeDtypeStruct(right_factor.shape, f32)
    left, made_momentum, made_right = pl.pallas_call(
        kernel,
        out_shape=(jax.ShapeDtypeStruct((rows, 3 * rank), bf16), new_momentum, new_right),
        in_specs=[pl.BlockSpec(memory_space=pltpu.HBM)] * 3,
        out_specs=[pl.BlockSpec(memory_space=pl.ANY)] * 3,
        scratch_shapes=[
            vm((rows, cols), bf16),
            vm((2, rows, cols), bf16),
            vm((rank, cols), f32),
            vm((rows, cols), bf16),
            vm((rows, cols), bf16),
            vm((4, 32, 128), f32),
            vm((8, 32, 128), f32),
            vm((4, 32, 128), f32),
            vm((4, 32, 128), f32),
            vm((16, 8, 128), f32),
            vm((16, 32, 128), f32),
            vm((5, 2, 32, 128), f32),
            vm((4, 32, 128), f32),
            vm((5, 32, 128), f32),
            vm((16, 32, 128), f32),
            vm((8, 2, 32, 128), f32),
            vm((16, 4, 128), f32),
            vm((16, 4, 128), f32),
            vm((16, 4, 128), f32),
            vm((8, 64, 128), f32),
            vm((4, 32, 128), f32),
            vm((4, 32, 128), f32),
            vm((4, 32, 128), f32),
            vm((4, 32, 128), f32),
            vm((64, 128), f32),
            vm((32, 8, 128), f32),
            vm((rows, 3 * rank), bf16),
            vm((rows, cols), bf16),
            vm((rank, cols), f32),
            pltpu.SemaphoreType.DMA((3,)),
            pltpu.SemaphoreType.DMA((3,)),
            pltpu.SemaphoreType.DMA((21,)),
            pltpu.SemaphoreType.DMA((21,)),
            pltpu.SemaphoreType.REGULAR((2,)),
        ],
        compiler_params=pltpu.CompilerParams(
            collective_id=0, has_side_effects=True, vmem_limit_bytes=63 * 1024 * 1024
        ),
        name="dion_step",
    )(momentum, grads, right_factor)
    parts = 4
    return pl.pallas_call(
        finish,
        out_shape=(new_weight, new_momentum, new_right),
        in_specs=[pl.BlockSpec(memory_space=pl.ANY)] * 4,
        out_specs=[pl.BlockSpec(memory_space=pl.ANY)] * 3,
        scratch_shapes=[
            vm((parts, rows // parts, cols), f32),
            vm((rows, 3 * rank), bf16),
            vm((1, rows, cols), bf16),
            vm((rank, cols), f32),
            pltpu.SemaphoreType.DMA((3 + parts,)),
            pltpu.SemaphoreType.DMA((2 + parts,)),
        ],
        compiler_params=pltpu.CompilerParams(vmem_limit_bytes=63 * 1024 * 1024),
        name="place",
    )(weight, left, made_momentum, made_right)


def solution(mesh):
    placed = (
        P("fsdp", "tensor"),
        P("dp", "fsdp", "tensor"),
        P("dp", None, "fsdp", "tensor"),
        P(None, "tensor"),
    )
    return jax.shard_map(
        local,
        mesh=mesh,
        in_specs=placed,
        out_specs=(P("fsdp", "tensor"), P("dp", "fsdp", "tensor"), P(None, "tensor")),
        check_vma=False,
    )
```

```python
import functools
import math

import jax
import jax.numpy as jnp
from jax import lax
from jax.experimental import pallas as pl
from jax.experimental.pallas import tpu as pltpu
from jax.sharding import PartitionSpec as P

ROWS = 4096
COLS = 4096

decay_part = 0.05
learn_rate = 0.02
epsilon = 1e-06

MESH = pl.DeviceIdType.MESH
f32 = jnp.float32
bf16 = jnp.bfloat16
NN = (((1,), (0,)), ((), ()))
NT = (((1,), (1,)), ((), ()))

AWAY = (0, 3, -3, 6, -6)


def split(x, n):
    parts = []
    for k in range(n):
        part = x.astype(bf16)
        parts.append(part)
        if k < n - 1:
            x = x - part.astype(f32)
    return parts


def dots(a, b, dims, order):
    total = None
    pairs = [(i, j) for i in range(len(a)) for j in range(len(b)) if i + j < order]
    for i, j in sorted(pairs, key=lambda t: -(t[0] + t[1])):
        term = lax.dot_general(a[i], b[j], dims, preferred_element_type=f32)
        total = term if total is None else total + term
    return total


def row_of(v, j):
    return jnp.broadcast_to(v[j : j + 1, :], (8, 128))


def lane_of(v, j):
    return jnp.broadcast_to(v[:, j : j + 1], (8, 128))


def eliminate(ref):
    sub = lax.broadcasted_iota(jnp.int32, (8, 128), 0)
    W = [ref[8 * i : 8 * i + 8, :] for i in range(8)]
    for kb in range(8):
        C = [[lane_of(w, 8 * kb + j) for j in range(8)] for w in W]
        Ls = [[None] * 8 for _ in W]
        R = W[0]
        us = []
        for j in range(8):
            r = lax.rsqrt(row_of(C[0][j], j))
            for i in range(len(W)):
                Ls[i][j] = C[i][j] * r
            u = row_of(R, j) * r
            us.append(u)
            R = R - Ls[0][j] * u
            for k in range(j + 1, 8):
                s = row_of(Ls[0][j], k)
                for i in range(len(W)):
                    C[i][k] = C[i][k] - Ls[i][j] * s
        U = us[0]
        for j in range(1, 8):
            U = jnp.where(sub == j, us[j], U)
        ref[8 * kb : 8 * kb + 8, :] = U
        rest = []
        for i in range(1, len(W)):
            w = W[i]
            for j in range(8):
                w = w - Ls[i][j] * us[j]
            rest.append(w)
        W = rest


def kernel(
    m_hbm, g_hbm, r_hbm, left_hbm, nm_hbm, nr_hbm, norm_hbm,
    m_v, g_v, r_v, bhi, blo,
    p_send, p_recv, px, pk, qk,
    rr, near, agg, far, rr_all, d_recv, sd, sd_recv, s_sub, s_all,
    gy, gx, hy, hx, aug, sq,
    left_v, nm_v, nr_v, norm_v,
    in_sem, out_sem, ssem, rsem, beyond,
):
    dp = lax.axis_index("dp")
    z = lax.axis_index("fsdp")
    x = lax.axis_index("tensor")
    y = dp // 2
    core = lax.bitwise_and(dp, 1)
    q = y * 4 + x

    def around(k):
        return lax.bitwise_and(z + (k + 16), 15)

    replicas = []
    for d in (4, 5, 2, 3, 6, 7, 1):
        o = lax.bitwise_xor(dp, d)
        replicas.append((o, {"dp": o}))
    ys, xs = [], []
    for d in (2, 1, 3):
        o = lax.bitwise_xor(y, d)
        ys.append((o, {"dp": o * 2 + core}))
        o = lax.bitwise_xor(x, d)
        xs.append((o, {"tensor": o}))

    barrier = pltpu.get_barrier_semaphore()
    greeted = [p for _, p in replicas] + [p for _, p in xs] + [{"fsdp": around(k)} for k in (2, -2, 1, -1)]
    for p in greeted:
        pl.semaphore_signal(barrier, inc=1, device_id=p, device_id_type=MESH)

    loads = [
        pltpu.make_async_copy(m_hbm.at[0], m_v, in_sem.at[0]),
        pltpu.make_async_copy(g_hbm.at[0], g_v, in_sem.at[1]),
        pltpu.make_async_copy(r_hbm, r_v, in_sem.at[2]),
    ]
    for load in loads:
        load.start()

    def tell(level, step):
        for k in (step, -step):
            pl.semaphore_signal(beyond.at[level], inc=1, device_id={"fsdp": around(k)}, device_id_type=MESH)

    def send(phase, src, dst, peer):
        pltpu.make_async_remote_copy(
            src_ref=src, dst_ref=dst, send_sem=ssem.at[phase], recv_sem=rsem.at[phase],
            device_id=peer, device_id_type=MESH,
        ).start()

    def arrived(phase, like):
        pltpu.make_async_copy(like, like, rsem.at[phase]).wait()

    def sent(phase, like):
        pltpu.make_async_copy(like, like, ssem.at[phase]).wait()

    loads[0].wait()
    loads[1].wait()
    loads[2].wait()
    rp = split(r_v[...], 2)
    halves = []
    for h in range(2):
        rows = slice(128 * h, 128 * h + 128)
        b = m_v[rows, :].astype(f32) + (g_v[0, rows, :].astype(f32) + g_v[1, rows, :].astype(f32))
        bp = split(b, 2)
        bhi[rows, :] = bp[0]
        blo[rows, :] = bp[1]
        halves.append(dots(bp, rp, NT, 2) * 0.125)
    p_send[...] = jnp.concatenate(halves, axis=1).reshape(4, 32, 128)

    pl.semaphore_wait(barrier, len(greeted))
    tell(0, 2)

    for o, peer in replicas:
        send(0, p_send.at[o // 2], p_recv.at[dp], peer)
    p_recv[dp] = p_send[y]
    pl.semaphore_wait(beyond.at[0], 2)
    tell(1, 4)
    arrived(0, p_recv.at[pl.ds(0, 7)])
    mine = p_recv[0]
    for k in range(1, 8):
        mine = mine + p_recv[k]
    px[x] = mine
    for o, peer in xs:
        send(1, px.at[x], px.at[x], peer)
    pl.semaphore_wait(beyond.at[1], 2)
    arrived(1, px.at[pl.ds(0, 3)])
    pk[y] = (px[0] + px[1]) + (px[2] + px[3])
    for o, peer in ys:
        send(2, pk.at[y], pk.at[y], peer)
    qk[z] = pk[y, pl.ds(pl.multiple_of(8 * x, 8), 8)]
    column = []
    for d in (8, 7, 9, 6, 10, 5, 11, 4, 12, 3, 13, 2, 14, 1, 15):
        o = around(d)
        column.append((o, {"fsdp": o}))
    for o, peer in column:
        send(3, qk.at[z], qk.at[z], peer)

    arrived(2, pk.at[pl.ds(0, 3)])
    pt = pk[...].reshape(128, 128).T
    pt = jnp.concatenate([pt[:64], pt[64:]], axis=1)
    ptp = split(pt, 3)
    for c in range(4):
        cols = slice(256 * c, 256 * c + 256)
        part = dots(ptp, [bhi[:, cols], blo[:, cols]], NN, 3)
        for k in range(2):
            for h in range(2):
                rr[4 * c + 2 * k + h] = part[32 * h : 32 * h + 32, 128 * k : 128 * k + 128]
    for o, peer in replicas:
        send(5, rr.at[pl.ds(2 * o, 2)], d_recv.at[dp], peer)
    for k in (3, 4, 1, 2, 0):
        for side, step in enumerate((1, -1)):
            o = around(step + AWAY[k])
            send(4 if k > 2 else 15, rr.at[o], near.at[k, side], {"fsdp": around(step)})
    send(16, rr.at[around(8)], far.at[0], {"fsdp": around(8)})
    d_recv[dp] = rr[pl.ds(2 * dp, 2)]

    def share_gram(t, first, second, phase):
        tp = split(t, 3)
        g = dots(tp, tp, NT, 3)
        first[y] = jnp.concatenate([g[:32], g[32:]], axis=1)
        for o, peer in ys:
            send(phase, first.at[y], first.at[y], peer)

    def pass_gram(first, second, phase):
        arrived(phase, first.at[pl.ds(0, 3)])
        second[x] = (first[0] + first[1]) + (first[2] + first[3])
        for o, peer in xs:
            send(phase + 1, second.at[x], second.at[x], peer)

    def whole_gram(second, phase):
        arrived(phase + 1, second.at[pl.ds(0, 3)])
        g = (second[0] + second[1]) + (second[2] + second[3])
        return jnp.concatenate([g, pltpu.roll(g, 64, 1)], axis=0)

    lanes = lax.broadcasted_iota(jnp.int32, (64, 128), 1)
    ranks = lax.broadcasted_iota(jnp.int32, (64, 128), 0)

    arrived(3, qk.at[pl.ds(0, 15)])
    qt = qk[...].reshape(128, 128).T
    qt = jnp.concatenate([qt[:64], qt[64:]], axis=1)
    share_gram(qt, gy, gx, 6)

    def forward(k):
        agg[k - 1] = rr[around(AWAY[k])] + near[k, 0] + near[k, 1]
        send(16, agg.at[k - 1], far.at[k], {"fsdp": around(AWAY[k])})

    pass_gram(gy, gx, 6)

    arrived(5, d_recv.at[pl.ds(0, 7)])
    total = d_recv[0]
    for k in range(1, 8):
        total = total + d_recv[k]
    total = total.reshape(64, 128)
    for k in range(16):
        sd[k] = total[4 * k : 4 * k + 4, :]
    for o, peer in column:
        send(10, sd.at[o], sd_recv.at[z], peer)
    sd_recv[z] = sd[z]
    arrived(4, near.at[pl.ds(3, 2)])
    forward(3)
    forward(4)
    arrived(15, near.at[pl.ds(0, 3)])
    forward(1)
    forward(2)

    g = whole_gram(gx, 6)
    aug[...] = jnp.where(lanes < 64, g, jnp.where(lanes == ranks + 64, 1.0, 0.0))
    eliminate(aug)
    first_inverse = aug[:, 64:]
    qt1 = dots(split(first_inverse, 3), split(qt, 3), NN, 3)
    share_gram(qt1, hy, hx, 8)

    arrived(10, sd_recv.at[pl.ds(0, 15)])
    total = sd_recv[0]
    for k in range(1, 16):
        total = total + sd_recv[k]
    s_sub[z] = total * 0.125
    for o, peer in column:
        send(12, s_sub.at[z], s_sub.at[z], peer)

    total = rr[z] + near[0, 0] + near[0, 1]
    arrived(16, far)
    for k in range(5):
        total = total + far[k]
    rr_all[z] = total
    for k in (3, 4, 1, 2):
        send(16 + k, rr_all.at[z], rr_all.at[z], {"fsdp": around(AWAY[k])})
    for step in (8, 1, -1):
        send(11, rr_all.at[z], rr_all.at[z], {"fsdp": around(step)})

    def hand_on(k):
        o = around(-AWAY[k])
        arrived(16 + k, rr_all.at[o])
        for step in (1, -1):
            send(11, rr_all.at[o], rr_all.at[o], {"fsdp": around(step)})

    pass_gram(hy, hx, 8)
    g = whole_gram(hx, 8)
    aug[...] = jnp.where(lanes < 64, g, aug[...])
    eliminate(aug)
    inverse = split(aug[:, 64:], 3)

    arrived(12, s_sub.at[pl.ds(0, 15)])
    for k in range(16):
        s_all[dp, 4 * k : 4 * k + 4, :] = s_sub[k]
    for o, peer in replicas:
        send(13, s_all.at[dp], s_all.at[dp], peer)
    shared = dots(inverse, split(s_all[dp], 3), NN, 3)
    sums = jnp.sum(shared * shared, axis=1, keepdims=True)
    small = lax.broadcasted_iota(jnp.int32, (8, 128), 1)
    tile = jnp.zeros((8, 128), f32)
    for i in range(8):
        tile = jnp.where(small == i, jnp.broadcast_to(sums[8 * i : 8 * i + 8], (8, 128)), tile)
    spot = core * 16 + q
    sq[spot] = tile
    everyone = []
    for d in (10, 9, 11, 6, 14, 2, 8, 5, 7, 13, 15, 1, 3, 4, 12, 0):
        o = lax.bitwise_xor(q, d)
        everyone.append({"dp": (o // 4) * 2 + 1 - core, "tensor": lax.bitwise_and(o, 3)})
        if d > 0:
            everyone.append({"dp": (o // 4) * 2 + core, "tensor": lax.bitwise_and(o, 3)})
    for peer in everyone:
        send(14, sq.at[spot], sq.at[spot], peer)

    for k in range(1, 5):
        hand_on(k)
    leftt = dots(inverse, ptp, NN, 3)
    lp = split(leftt, 2)
    l0 = lp[0].astype(f32)
    l1 = lp[1].astype(f32)
    left3 = jnp.concatenate([l0, l0, l1], axis=0).T.astype(bf16)
    left_v[...] = left3
    left_out = pltpu.make_async_copy(left_v, left_hbm, out_sem.at[2])
    left_out.start()

    arrived(11, rr_all.at[pl.ds(0, 11)])
    for c in range(4):
        cols = slice(256 * c, 256 * c + 256)
        raw = jnp.concatenate(
            [jnp.concatenate([rr_all[4 * c + h], rr_all[4 * c + 2 + h]], axis=1) for h in range(2)], axis=0
        )
        right = dots(inverse, split(raw, 3), NN, 3)
        r0, r1 = split(right, 2)
        right3 = jnp.concatenate([r0, r1, r0], axis=0)
        projected = lax.dot_general(left3, right3, NN, preferred_element_type=f32)
        b = m_v[:, cols].astype(f32) + (g_v[0, :, cols].astype(f32) + g_v[1, :, cols].astype(f32))
        nm_v[:, cols] = (b - decay_part * projected).astype(bf16)
    nm_out = pltpu.make_async_copy(nm_v, nm_hbm.at[0], out_sem.at[0])
    nm_out.start()

    arrived(13, s_all.at[pl.ds(0, 7)])
    for k in range(8):
        nr_v[:, 128 * k : 128 * k + 128] = dots(inverse, split(s_all[k], 3), NN, 3)
    nr_out = pltpu.make_async_copy(nr_v, nr_hbm, out_sem.at[1])
    nr_out.start()
    arrived(14, sq.at[pl.ds(0, 31)])
    tile = sq[0]
    for k in range(1, 32):
        tile = tile + sq[k]
    norm_v[...] = 1.0 / jnp.sqrt(tile + epsilon)
    norm_out = pltpu.make_async_copy(norm_v, norm_hbm, out_sem.at[3])
    norm_out.start()

    sent(0, p_recv.at[pl.ds(0, 7)])
    sent(1, px.at[pl.ds(0, 3)])
    sent(2, pk.at[pl.ds(0, 3)])
    sent(3, qk.at[pl.ds(0, 15)])
    sent(4, rr.at[pl.ds(0, 4)])
    sent(15, rr.at[pl.ds(0, 6)])
    sent(16, far)
    for k in range(1, 5):
        sent(16 + k, rr_all.at[0])
    sent(5, d_recv.at[pl.ds(0, 7)])
    sent(6, gy.at[pl.ds(0, 3)])
    sent(7, gx.at[pl.ds(0, 3)])
    sent(8, hy.at[pl.ds(0, 3)])
    sent(9, hx.at[pl.ds(0, 3)])
    sent(10, sd.at[pl.ds(0, 15)])
    sent(11, rr_all.at[pl.ds(0, 11)])
    sent(12, s_sub.at[pl.ds(0, 15)])
    sent(13, s_all.at[pl.ds(0, 7)])
    sent(14, sq.at[pl.ds(0, 31)])
    nm_out.wait()
    nr_out.wait()
    left_out.wait()
    norm_out.wait()


def finish(
    w_hbm, left_hbm, nm_in, nr_in, norm_in, nw_out, nm_out, nr_out,
    w_v, left_v, nm_v, nr_v, norm_v, isem, osem,
):
    rows = w_v.shape[1]
    parts = range(w_v.shape[0])
    reads = [
        pltpu.make_async_copy(nr_in, nr_v, isem.at[0]),
        pltpu.make_async_copy(left_hbm, left_v, isem.at[1]),
    ]
    reads += [pltpu.make_async_copy(w_hbm.at[pl.ds(rows * k, rows)], w_v.at[k], isem.at[3 + k]) for k in parts]
    reads.append(pltpu.make_async_copy(nm_in, nm_v, isem.at[2]))
    norm = pltpu.make_async_copy(norm_in, norm_v, isem.at[3 + len(parts)])
    norm.start()
    for read in reads:
        read.start()
    norm.wait()
    tile = norm_v[...]
    factor = jnp.concatenate([lane_of(tile, i) for i in range(8)], axis=0)
    reads[0].wait()
    for k in range(nr_v.shape[1] // 128):
        nr_v[:, 128 * k : 128 * k + 128] = nr_v[:, 128 * k : 128 * k + 128] * factor
    writes = [pltpu.make_async_copy(nr_v, nr_out, osem.at[0])]
    writes[0].start()
    scale = learn_rate * math.sqrt(ROWS / COLS)
    r0, r1 = split(nr_v[...], 2)
    right3 = jnp.concatenate([r0, r1, r0], axis=0)
    reads[1].wait()
    for k in parts:
        reads[2 + k].wait()
        step = lax.dot_general(left_v[rows * k : rows * k + rows], right3, NN, preferred_element_type=f32)
        w_v[k] = w_v[k] - scale * step
        writes.append(pltpu.make_async_copy(w_v.at[k], nw_out.at[pl.ds(rows * k, rows)], osem.at[2 + k]))
        writes[-1].start()
    reads[-1].wait()
    writes.append(pltpu.make_async_copy(nm_v, nm_out, osem.at[1]))
    writes[-1].start()
    for write in writes:
        write.wait()


def local(weight, momentum, grads, right_factor):
    rows, cols = weight.shape
    rank = right_factor.shape[0]
    vm = pltpu.VMEM
    new_weight = jax.ShapeDtypeStruct(weight.shape, f32)
    new_momentum = jax.ShapeDtypeStruct(momentum.shape, bf16)
    new_right = jax.ShapeDtypeStruct(right_factor.shape, f32)
    left, made_momentum, made_right, norm = pl.pallas_call(
        kernel,
        out_shape=(jax.ShapeDtypeStruct((rows, 3 * rank), bf16), new_momentum, new_right, jax.ShapeDtypeStruct((8, 128), f32)),
        in_specs=[pl.BlockSpec(memory_space=pltpu.HBM)] * 3,
        out_specs=[pl.BlockSpec(memory_space=pl.ANY)] * 4,
        scratch_shapes=[
            vm((rows, cols), bf16),
            vm((2, rows, cols), bf16),
            vm((rank, cols), f32),
            vm((rows, cols), bf16),
            vm((rows, cols), bf16),
            vm((4, 32, 128), f32),
            vm((8, 32, 128), f32),
            vm((4, 32, 128), f32),
            vm((4, 32, 128), f32),
            vm((16, 8, 128), f32),
            vm((16, 32, 128), f32),
            vm((5, 2, 32, 128), f32),
            vm((4, 32, 128), f32),
            vm((5, 32, 128), f32),
            vm((16, 32, 128), f32),
            vm((8, 2, 32, 128), f32),
            vm((16, 4, 128), f32),
            vm((16, 4, 128), f32),
            vm((16, 4, 128), f32),
            vm((8, 64, 128), f32),
            vm((4, 32, 128), f32),
            vm((4, 32, 128), f32),
            vm((4, 32, 128), f32),
            vm((4, 32, 128), f32),
            vm((64, 128), f32),
            vm((32, 8, 128), f32),
            vm((rows, 3 * rank), bf16),
            vm((rows, cols), bf16),
            vm((rank, cols), f32),
            vm((8, 128), f32),
            pltpu.SemaphoreType.DMA((3,)),
            pltpu.SemaphoreType.DMA((4,)),
            pltpu.SemaphoreType.DMA((21,)),
            pltpu.SemaphoreType.DMA((21,)),
            pltpu.SemaphoreType.REGULAR((2,)),
        ],
        compiler_params=pltpu.CompilerParams(
            collective_id=0, has_side_effects=True, vmem_limit_bytes=63 * 1024 * 1024
        ),
        name="dion_step",
    )(momentum, grads, right_factor)
    parts = 4
    return pl.pallas_call(
        finish,
        out_shape=(new_weight, new_momentum, new_right),
        in_specs=[pl.BlockSpec(memory_space=pl.ANY)] * 5,
        out_specs=[pl.BlockSpec(memory_space=pl.ANY)] * 3,
        scratch_shapes=[
            vm((parts, rows // parts, cols), f32),
            vm((rows, 3 * rank), bf16),
            vm((1, rows, cols), bf16),
            vm((rank, cols), f32),
            vm((8, 128), f32),
            pltpu.SemaphoreType.DMA((4 + parts,)),
            pltpu.SemaphoreType.DMA((2 + parts,)),
        ],
        compiler_params=pltpu.CompilerParams(vmem_limit_bytes=63 * 1024 * 1024),
        name="place",
    )(weight, left, made_momentum, made_right, norm)


def solution(mesh):
    placed = (
        P("fsdp", "tensor"),
        P("dp", "fsdp", "tensor"),
        P("dp", None, "fsdp", "tensor"),
        P(None, "tensor"),
    )
    return jax.shard_map(
        local,
        mesh=mesh,
        in_specs=placed,
        out_specs=(P("fsdp", "tensor"), P("dp", "fsdp", "tensor"), P(None, "tensor")),
        check_vma=False,
    )
```

```python
import functools
import math

import jax
import jax.numpy as jnp
from jax import lax
from jax.experimental import pallas as pl
from jax.experimental.pallas import tpu as pltpu
from jax.sharding import PartitionSpec as P

ROWS = 4096
COLS = 4096

decay_part = 0.05
learn_rate = 0.02
epsilon = 1e-06

MESH = pl.DeviceIdType.MESH
f32 = jnp.float32
bf16 = jnp.bfloat16
NN = (((1,), (0,)), ((), ()))
NT = (((1,), (1,)), ((), ()))

AWAY = (0, 3, -3, 6, -6)


def split(x, n):
    parts = []
    for k in range(n):
        part = x.astype(bf16)
        parts.append(part)
        if k < n - 1:
            x = x - part.astype(f32)
    return parts


def dots(a, b, dims, order):
    total = None
    pairs = [(i, j) for i in range(len(a)) for j in range(len(b)) if i + j < order]
    for i, j in sorted(pairs, key=lambda t: -(t[0] + t[1])):
        term = lax.dot_general(a[i], b[j], dims, preferred_element_type=f32)
        total = term if total is None else total + term
    return total


def row_of(v, j):
    return jnp.broadcast_to(v[j : j + 1, :], (8, 128))


def lane_of(v, j):
    return jnp.broadcast_to(v[:, j : j + 1], (8, 128))


def eliminate(ref):
    sub = lax.broadcasted_iota(jnp.int32, (8, 128), 0)
    W = [ref[8 * i : 8 * i + 8, :] for i in range(8)]
    for kb in range(8):
        C = [[lane_of(w, 8 * kb + j) for j in range(8)] for w in W]
        Ls = [[None] * 8 for _ in W]
        R = W[0]
        us = []
        for j in range(8):
            r = lax.rsqrt(row_of(C[0][j], j))
            for i in range(len(W)):
                Ls[i][j] = C[i][j] * r
            u = row_of(R, j) * r
            us.append(u)
            R = R - Ls[0][j] * u
            for k in range(j + 1, 8):
                s = row_of(Ls[0][j], k)
                for i in range(len(W)):
                    C[i][k] = C[i][k] - Ls[i][j] * s
        U = us[0]
        for j in range(1, 8):
            U = jnp.where(sub == j, us[j], U)
        ref[8 * kb : 8 * kb + 8, :] = U
        rest = []
        for i in range(1, len(W)):
            w = W[i]
            for j in range(8):
                w = w - Ls[i][j] * us[j]
            rest.append(w)
        W = rest


def kernel(
    m_hbm, g_hbm, r_hbm, left_hbm, nm_hbm, nr_hbm, norm_hbm,
    m_v, g_v, r_v, bhi, blo,
    p_send, p_recv, px, pk, qk,
    rr, near, agg, far, rr_all, d_recv, sd, sd_recv, s_sub, s_all,
    gy, gx, hy, hx, aug, sq,
    left_v, nm_v, nr_v, norm_v,
    in_sem, out_sem, ssem, rsem, beyond,
):
    dp = lax.axis_index("dp")
    z = lax.axis_index("fsdp")
    x = lax.axis_index("tensor")
    y = dp // 2
    core = lax.bitwise_and(dp, 1)
    q = y * 4 + x

    def around(k):
        return lax.bitwise_and(z + (k + 16), 15)

    replicas = []
    for d in (4, 5, 2, 3, 6, 7, 1):
        o = lax.bitwise_xor(dp, d)
        replicas.append((o, {"dp": o}))
    ys, xs = [], []
    for d in (2, 1, 3):
        o = lax.bitwise_xor(y, d)
        ys.append((o, {"dp": o * 2 + core}))
        o = lax.bitwise_xor(x, d)
        xs.append((o, {"tensor": o}))

    barrier = pltpu.get_barrier_semaphore()
    greeted = [p for _, p in replicas] + [p for _, p in xs] + [{"fsdp": around(k)} for k in (2, -2, 1, -1)]
    for p in greeted:
        pl.semaphore_signal(barrier, inc=1, device_id=p, device_id_type=MESH)

    loads = [
        pltpu.make_async_copy(m_hbm.at[0], m_v, in_sem.at[0]),
        pltpu.make_async_copy(g_hbm.at[0], g_v, in_sem.at[1]),
        pltpu.make_async_copy(r_hbm, r_v, in_sem.at[2]),
    ]
    for load in loads:
        load.start()

    def tell(level, step):
        for k in (step, -step):
            pl.semaphore_signal(beyond.at[level], inc=1, device_id={"fsdp": around(k)}, device_id_type=MESH)

    def send(phase, src, dst, peer):
        pltpu.make_async_remote_copy(
            src_ref=src, dst_ref=dst, send_sem=ssem.at[phase], recv_sem=rsem.at[phase],
            device_id=peer, device_id_type=MESH,
        ).start()

    def arrived(phase, like):
        pltpu.make_async_copy(like, like, rsem.at[phase]).wait()

    def sent(phase, like):
        pltpu.make_async_copy(like, like, ssem.at[phase]).wait()

    loads[0].wait()
    loads[1].wait()
    loads[2].wait()
    rp = split(r_v[...], 2)
    halves = []
    for h in range(2):
        rows = slice(128 * h, 128 * h + 128)
        b = m_v[rows, :].astype(f32) + (g_v[0, rows, :].astype(f32) + g_v[1, rows, :].astype(f32))
        bp = split(b, 2)
        bhi[rows, :] = bp[0]
        blo[rows, :] = bp[1]
        halves.append(dots(bp, rp, NT, 2) * 0.125)
    p_send[...] = jnp.concatenate(halves, axis=1).reshape(4, 32, 128)

    pl.semaphore_wait(barrier, len(greeted))
    tell(0, 2)

    for o, peer in replicas:
        send(0, p_send.at[o // 2], p_recv.at[dp], peer)
    p_recv[dp] = p_send[y]
    pl.semaphore_wait(beyond.at[0], 2)
    tell(1, 4)
    arrived(0, p_recv.at[pl.ds(0, 7)])
    mine = p_recv[0]
    for k in range(1, 8):
        mine = mine + p_recv[k]
    px[x] = mine
    for o, peer in xs:
        send(1, px.at[x], px.at[x], peer)
    pl.semaphore_wait(beyond.at[1], 2)
    arrived(1, px.at[pl.ds(0, 3)])
    pk[y] = (px[0] + px[1]) + (px[2] + px[3])
    for o, peer in ys:
        send(2, pk.at[y], pk.at[y], peer)
    qk[z] = pk[y, pl.ds(pl.multiple_of(8 * x, 8), 8)]
    column = []
    for d in (8, 7, 9, 6, 10, 5, 11, 4, 12, 3, 13, 2, 14, 1, 15):
        o = around(d)
        column.append((o, {"fsdp": o}))
    for o, peer in column:
        send(3, qk.at[z], qk.at[z], peer)

    arrived(2, pk.at[pl.ds(0, 3)])
    pt = pk[...].reshape(128, 128).T
    pt = jnp.concatenate([pt[:64], pt[64:]], axis=1)
    ptp = split(pt, 3)
    for c in range(4):
        cols = slice(256 * c, 256 * c + 256)
        part = dots(ptp, [bhi[:, cols], blo[:, cols]], NN, 3)
        for k in range(2):
            for h in range(2):
                rr[4 * c + 2 * k + h] = part[32 * h : 32 * h + 32, 128 * k : 128 * k + 128]
    for o, peer in replicas:
        send(5, rr.at[pl.ds(2 * o, 2)], d_recv.at[dp], peer)
    for k in (3, 4, 1, 2, 0):
        for side, step in enumerate((1, -1)):
            o = around(step + AWAY[k])
            send(4 if k > 2 else 15, rr.at[o], near.at[k, side], {"fsdp": around(step)})
    send(16, rr.at[around(8)], far.at[0], {"fsdp": around(8)})
    d_recv[dp] = rr[pl.ds(2 * dp, 2)]

    def share_gram(t, first, second, phase, order):
        tp = split(t, order)
        g = dots(tp, tp, NT, order)
        first[y] = jnp.concatenate([g[:32], g[32:]], axis=1)
        for o, peer in ys:
            send(phase, first.at[y], first.at[y], peer)

    def pass_gram(first, second, phase):
        arrived(phase, first.at[pl.ds(0, 3)])
        second[x] = (first[0] + first[1]) + (first[2] + first[3])
        for o, peer in xs:
            send(phase + 1, second.at[x], second.at[x], peer)

    def whole_gram(second, phase):
        arrived(phase + 1, second.at[pl.ds(0, 3)])
        g = (second[0] + second[1]) + (second[2] + second[3])
        return jnp.concatenate([g, pltpu.roll(g, 64, 1)], axis=0)

    lanes = lax.broadcasted_iota(jnp.int32, (64, 128), 1)
    ranks = lax.broadcasted_iota(jnp.int32, (64, 128), 0)

    arrived(3, qk.at[pl.ds(0, 15)])
    qt = qk[...].reshape(128, 128).T
    qt = jnp.concatenate([qt[:64], qt[64:]], axis=1)
    share_gram(qt, gy, gx, 6, 3)

    def forward(k):
        agg[k - 1] = rr[around(AWAY[k])] + near[k, 0] + near[k, 1]
        send(16, agg.at[k - 1], far.at[k], {"fsdp": around(AWAY[k])})

    pass_gram(gy, gx, 6)

    arrived(5, d_recv.at[pl.ds(0, 7)])
    total = d_recv[0]
    for k in range(1, 8):
        total = total + d_recv[k]
    total = total.reshape(64, 128)
    for k in range(16):
        sd[k] = total[4 * k : 4 * k + 4, :]
    for o, peer in column:
        send(10, sd.at[o], sd_recv.at[z], peer)
    sd_recv[z] = sd[z]
    arrived(4, near.at[pl.ds(3, 2)])
    forward(3)
    forward(4)
    arrived(15, near.at[pl.ds(0, 3)])
    forward(1)
    forward(2)

    g = whole_gram(gx, 6)
    aug[...] = jnp.where(lanes < 64, g, jnp.where(lanes == ranks + 64, 1.0, 0.0))
    eliminate(aug)
    first_inverse = aug[:, 64:]
    qt1 = dots(split(first_inverse, 3), split(qt, 3), NN, 3)
    share_gram(qt1, hy, hx, 8, 2)

    arrived(10, sd_recv.at[pl.ds(0, 15)])
    total = sd_recv[0]
    for k in range(1, 16):
        total = total + sd_recv[k]
    s_sub[z] = total * 0.125
    for o, peer in column:
        send(12, s_sub.at[z], s_sub.at[z], peer)

    total = rr[z] + near[0, 0] + near[0, 1]
    arrived(16, far)
    for k in range(5):
        total = total + far[k]
    rr_all[z] = total
    for k in (3, 4, 1, 2):
        send(16 + k, rr_all.at[z], rr_all.at[z], {"fsdp": around(AWAY[k])})
    for step in (8, 1, -1):
        send(11, rr_all.at[z], rr_all.at[z], {"fsdp": around(step)})

    def hand_on(k):
        o = around(-AWAY[k])
        arrived(16 + k, rr_all.at[o])
        for step in (1, -1):
            send(11, rr_all.at[o], rr_all.at[o], {"fsdp": around(step)})

    pass_gram(hy, hx, 8)
    g = whole_gram(hx, 8)
    aug[...] = jnp.where(lanes < 64, g, aug[...])
    eliminate(aug)
    inverse = split(aug[:, 64:], 3)

    arrived(12, s_sub.at[pl.ds(0, 15)])
    for k in range(16):
        s_all[dp, 4 * k : 4 * k + 4, :] = s_sub[k]
    for o, peer in replicas:
        send(13, s_all.at[dp], s_all.at[dp], peer)
    shared = dots(inverse, split(s_all[dp], 3), NN, 3)
    sums = jnp.sum(shared * shared, axis=1, keepdims=True)
    small = lax.broadcasted_iota(jnp.int32, (8, 128), 1)
    tile = jnp.zeros((8, 128), f32)
    for i in range(8):
        tile = jnp.where(small == i, jnp.broadcast_to(sums[8 * i : 8 * i + 8], (8, 128)), tile)
    spot = core * 16 + q
    sq[spot] = tile
    everyone = []
    for d in (10, 9, 11, 6, 14, 2, 8, 5, 7, 13, 15, 1, 3, 4, 12, 0):
        o = lax.bitwise_xor(q, d)
        everyone.append({"dp": (o // 4) * 2 + 1 - core, "tensor": lax.bitwise_and(o, 3)})
        if d > 0:
            everyone.append({"dp": (o // 4) * 2 + core, "tensor": lax.bitwise_and(o, 3)})
    for peer in everyone:
        send(14, sq.at[spot], sq.at[spot], peer)

    for k in range(1, 5):
        hand_on(k)
    leftt = dots(inverse, ptp, NN, 3)
    lp = split(leftt, 2)
    l0 = lp[0].astype(f32)
    l1 = lp[1].astype(f32)
    left3 = jnp.concatenate([l0, l0, l1], axis=0).T.astype(bf16)
    left_v[...] = left3
    left_out = pltpu.make_async_copy(left_v, left_hbm, out_sem.at[2])
    left_out.start()

    arrived(11, rr_all.at[pl.ds(0, 11)])
    for c in range(4):
        cols = slice(256 * c, 256 * c + 256)
        raw = jnp.concatenate(
            [jnp.concatenate([rr_all[4 * c + h], rr_all[4 * c + 2 + h]], axis=1) for h in range(2)], axis=0
        )
        right = dots(inverse, split(raw, 3), NN, 3)
        r0, r1 = split(right, 2)
        right3 = jnp.concatenate([r0, r1, r0], axis=0)
        projected = lax.dot_general(left3, right3, NN, preferred_element_type=f32)
        b = m_v[:, cols].astype(f32) + (g_v[0, :, cols].astype(f32) + g_v[1, :, cols].astype(f32))
        nm_v[:, cols] = (b - decay_part * projected).astype(bf16)
    nm_out = pltpu.make_async_copy(nm_v, nm_hbm.at[0], out_sem.at[0])
    nm_out.start()

    arrived(13, s_all.at[pl.ds(0, 7)])
    for k in range(8):
        nr_v[:, 128 * k : 128 * k + 128] = dots(inverse, split(s_all[k], 3), NN, 3)
    nr_out = pltpu.make_async_copy(nr_v, nr_hbm, out_sem.at[1])
    nr_out.start()
    arrived(14, sq.at[pl.ds(0, 31)])
    tile = sq[0]
    for k in range(1, 32):
        tile = tile + sq[k]
    norm_v[...] = 1.0 / jnp.sqrt(tile + epsilon)
    norm_out = pltpu.make_async_copy(norm_v, norm_hbm, out_sem.at[3])
    norm_out.start()

    sent(0, p_recv.at[pl.ds(0, 7)])
    sent(1, px.at[pl.ds(0, 3)])
    sent(2, pk.at[pl.ds(0, 3)])
    sent(3, qk.at[pl.ds(0, 15)])
    sent(4, rr.at[pl.ds(0, 4)])
    sent(15, rr.at[pl.ds(0, 6)])
    sent(16, far)
    for k in range(1, 5):
        sent(16 + k, rr_all.at[0])
    sent(5, d_recv.at[pl.ds(0, 7)])
    sent(6, gy.at[pl.ds(0, 3)])
    sent(7, gx.at[pl.ds(0, 3)])
    sent(8, hy.at[pl.ds(0, 3)])
    sent(9, hx.at[pl.ds(0, 3)])
    sent(10, sd.at[pl.ds(0, 15)])
    sent(11, rr_all.at[pl.ds(0, 11)])
    sent(12, s_sub.at[pl.ds(0, 15)])
    sent(13, s_all.at[pl.ds(0, 7)])
    sent(14, sq.at[pl.ds(0, 31)])
    nm_out.wait()
    nr_out.wait()
    left_out.wait()
    norm_out.wait()


def finish(
    w_hbm, left_hbm, nm_in, nr_in, norm_in, nw_out, nm_out, nr_out,
    w_v, left_v, nm_v, nr_v, norm_v, isem, osem,
):
    rows = w_v.shape[1]
    parts = range(w_v.shape[0])
    reads = [
        pltpu.make_async_copy(nr_in, nr_v, isem.at[0]),
        pltpu.make_async_copy(left_hbm, left_v, isem.at[1]),
    ]
    reads += [pltpu.make_async_copy(w_hbm.at[pl.ds(rows * k, rows)], w_v.at[k], isem.at[3 + k]) for k in parts]
    reads.append(pltpu.make_async_copy(nm_in, nm_v, isem.at[2]))
    norm = pltpu.make_async_copy(norm_in, norm_v, isem.at[3 + len(parts)])
    norm.start()
    for read in reads:
        read.start()
    norm.wait()
    tile = norm_v[...]
    factor = jnp.concatenate([lane_of(tile, i) for i in range(8)], axis=0)
    reads[0].wait()
    for k in range(nr_v.shape[1] // 128):
        nr_v[:, 128 * k : 128 * k + 128] = nr_v[:, 128 * k : 128 * k + 128] * factor
    writes = [pltpu.make_async_copy(nr_v, nr_out, osem.at[0])]
    writes[0].start()
    scale = learn_rate * math.sqrt(ROWS / COLS)
    r0, r1 = split(nr_v[...], 2)
    right3 = jnp.concatenate([r0, r1, r0], axis=0)
    reads[1].wait()
    for k in parts:
        reads[2 + k].wait()
        step = lax.dot_general(left_v[rows * k : rows * k + rows], right3, NN, preferred_element_type=f32)
        w_v[k] = w_v[k] - scale * step
        writes.append(pltpu.make_async_copy(w_v.at[k], nw_out.at[pl.ds(rows * k, rows)], osem.at[2 + k]))
        writes[-1].start()
    reads[-1].wait()
    writes.append(pltpu.make_async_copy(nm_v, nm_out, osem.at[1]))
    writes[-1].start()
    for write in writes:
        write.wait()


def local(weight, momentum, grads, right_factor):
    rows, cols = weight.shape
    rank = right_factor.shape[0]
    vm = pltpu.VMEM
    new_weight = jax.ShapeDtypeStruct(weight.shape, f32)
    new_momentum = jax.ShapeDtypeStruct(momentum.shape, bf16)
    new_right = jax.ShapeDtypeStruct(right_factor.shape, f32)
    left, made_momentum, made_right, norm = pl.pallas_call(
        kernel,
        out_shape=(jax.ShapeDtypeStruct((rows, 3 * rank), bf16), new_momentum, new_right, jax.ShapeDtypeStruct((8, 128), f32)),
        in_specs=[pl.BlockSpec(memory_space=pltpu.HBM)] * 3,
        out_specs=[pl.BlockSpec(memory_space=pl.ANY)] * 4,
        scratch_shapes=[
            vm((rows, cols), bf16),
            vm((2, rows, cols), bf16),
            vm((rank, cols), f32),
            vm((rows, cols), bf16),
            vm((rows, cols), bf16),
            vm((4, 32, 128), f32),
            vm((8, 32, 128), f32),
            vm((4, 32, 128), f32),
            vm((4, 32, 128), f32),
            vm((16, 8, 128), f32),
            vm((16, 32, 128), f32),
            vm((5, 2, 32, 128), f32),
            vm((4, 32, 128), f32),
            vm((5, 32, 128), f32),
            vm((16, 32, 128), f32),
            vm((8, 2, 32, 128), f32),
            vm((16, 4, 128), f32),
            vm((16, 4, 128), f32),
            vm((16, 4, 128), f32),
            vm((8, 64, 128), f32),
            vm((4, 32, 128), f32),
            vm((4, 32, 128), f32),
            vm((4, 32, 128), f32),
            vm((4, 32, 128), f32),
            vm((64, 128), f32),
            vm((32, 8, 128), f32),
            vm((rows, 3 * rank), bf16),
            vm((rows, cols), bf16),
            vm((rank, cols), f32),
            vm((8, 128), f32),
            pltpu.SemaphoreType.DMA((3,)),
            pltpu.SemaphoreType.DMA((4,)),
            pltpu.SemaphoreType.DMA((21,)),
            pltpu.SemaphoreType.DMA((21,)),
            pltpu.SemaphoreType.REGULAR((2,)),
        ],
        compiler_params=pltpu.CompilerParams(
            collective_id=0, has_side_effects=True, vmem_limit_bytes=63 * 1024 * 1024
        ),
        name="dion_step",
    )(momentum, grads, right_factor)
    parts = 4
    return pl.pallas_call(
        finish,
        out_shape=(new_weight, new_momentum, new_right),
        in_specs=[pl.BlockSpec(memory_space=pl.ANY)] * 5,
        out_specs=[pl.BlockSpec(memory_space=pl.ANY)] * 3,
        scratch_shapes=[
            vm((parts, rows // parts, cols), f32),
            vm((rows, 3 * rank), bf16),
            vm((1, rows, cols), bf16),
            vm((rank, cols), f32),
            vm((8, 128), f32),
            pltpu.SemaphoreType.DMA((4 + parts,)),
            pltpu.SemaphoreType.DMA((2 + parts,)),
        ],
        compiler_params=pltpu.CompilerParams(vmem_limit_bytes=63 * 1024 * 1024),
        name="place",
    )(weight, left, made_momentum, made_right, norm)


def solution(mesh):
    placed = (
        P("fsdp", "tensor"),
        P("dp", "fsdp", "tensor"),
        P("dp", None, "fsdp", "tensor"),
        P(None, "tensor"),
    )
    return jax.shard_map(
        local,
        mesh=mesh,
        in_specs=placed,
        out_specs=(P("fsdp", "tensor"), P("dp", "fsdp", "tensor"), P(None, "tensor")),
        check_vma=False,
    )
```
